32 devices in a mesh: kv: 4 (over y, x), seq: 8 (over z, core).
Axes of the slice: x: 2, y: 2, z: 4, core: 2. Of those that a mesh axis runs over, the one named last changes fastest.
Arguments:
- page_cache: bfloat16 [512, 2, 8, 128, 128], P('seq', None, 'kv'), may hold values from -9 to 64
- keep_list: int32 [512, 128], P('seq'), may hold values from 0 to 1, as said below
- fold_weight: float32 [512, 128], P('seq'), may hold values from 0.1 to 10
- page_table: int32 [64, 8], replicated, may hold values from 0 to 511, as said below
- lengths: int32 [64], replicated, may hold values from 1 to 1024, 40960 in all
- queries: bfloat16 [64, 16, 128], P('seq', 'kv'), may hold values from -6 to 40
- fresh_entries: bfloat16 [64, 2, 8, 128], P('seq', None, 'kv'), may hold values from -6 to 6
- out_weight: bfloat16 [2048, 2048], P('kv'), may hold values from -0.125 to 0.125
Outputs:
- packed_cache: bfloat16 [512, 2, 8, 128, 128], P('seq', None, 'kv')
- packed_mass: bfloat16 [512, 128], P('seq')
- attended: bfloat16 [64, 2048], P('seq', 'kv')
- projected: bfloat16 [64, 2048], P('seq', 'kv')
The draws below stay inside these ranges and needn't reach their ends.
Inputs may be any that keep to these rules, and one draw needn't show every extreme that they name: `page_table`: every physical page appears exactly once. Of the 64 pages of the requests held by one index of seq, exactly 8 lie on each index of seq. `keep_list`: every page keeps at least one and drops at least one of its 128 slots.
All inputs are finite; a program needn't handle non-finite values.
Results may differ from the reference program's by a relative error of at most 0.015.
Values may be sent and summed in bfloat16 or wider, within the bound.
No kernel may reach another device: no remote copies, remote signals or barrier semaphores. Data moves between devices by JAX's collectives and lax.ppermute only.
A program may use at most 128 MiB of HBM per device.

```python
import math
import jax
import jax.numpy as jnp
import numpy as np
from jax import lax

D = 2048
HQ = 16
KVH = 8
HD = 128
PSZ = 128
MAXP = 8
PD = 64
PAGES = 512
REQS = 64


def draw_page_table(key, part):
    seq_count = PAGES // PD
    peer_pages = PD // seq_count
    base = jnp.repeat(jnp.arange(seq_count, dtype=jnp.int32), peer_pages)
    source_keys = jax.random.split(jax.random.fold_in(key, 11), seq_count)
    holder = jax.vmap(lambda one: jax.random.permutation(one, base))(source_keys)
    earlier = jnp.arange(PD)[None, :] < jnp.arange(PD)[:, None]
    same = holder[:, :, None] == holder[:, None, :]
    within = jnp.sum(jnp.logical_and(same, earlier[None]), axis=2).astype(jnp.int32)
    order_rank = jnp.arange(seq_count, dtype=jnp.int32)[:, None] * peer_pages + within
    slot_keys = jax.random.split(jax.random.fold_in(key, 12), seq_count)
    slot_perm = jax.vmap(lambda one: jax.random.permutation(one, PD))(slot_keys).astype(jnp.int32)
    slot = slot_perm[holder, order_rank]
    physical = holder * PD + slot
    return physical.reshape(REQS, MAXP).astype(jnp.int32)


def draw_keep_list(key, part):
    first, second, third, fourth = jax.random.split(jax.random.fold_in(key, 21), 4)
    level = jax.random.randint(first, (PAGES, 1), 16, 112)
    ticket = jax.random.randint(second, (PAGES, PSZ), 0, 128)
    keep_mask = ticket < level
    forced_keep = jax.random.randint(third, (PAGES, 1), 0, PSZ)
    offset = jax.random.randint(fourth, (PAGES, 1), 1, PSZ)
    forced_drop = (forced_keep + offset) % PSZ
    slot_index = jnp.arange(PSZ)[None, :]
    keep_mask = jnp.where(slot_index == forced_keep, True, keep_mask)
    keep_mask = jnp.where(slot_index == forced_drop, False, keep_mask)
    return keep_mask.astype(jnp.int32)


def draw_queries(key, part):
    shape = (REQS, HQ, HD)
    values = jnp.clip(jax.random.normal(jax.random.fold_in(key, 32), shape, jnp.float32), -6.0, 6.0)
    return values.astype(jnp.bfloat16)


def draw_page_cache(key, part):
    shape = (PAGES, 2, KVH, PSZ, HD)
    key_mask = (jnp.arange(2) == 0).reshape(1, 2, 1, 1, 1)
    noise = jnp.clip(jax.random.normal(jax.random.fold_in(key, 42), shape, jnp.float32), -6.0, 6.0)
    values = noise * jnp.where(key_mask, 1.5, 1.0)
    return values.astype(jnp.bfloat16)


def steps_of(own_key, dims, pieces, least, largest):
    gain = 1.0
    for dim, shards_of in pieces:
        heights = jax.random.uniform(jax.random.fold_in(jax.random.fold_in(own_key, 6), dim), (shards_of,), jnp.float32, least / len(pieces), largest / len(pieces))
        gain = gain * jnp.repeat(jnp.exp(heights), dims[dim] // shards_of).reshape((-1,) + (1,) * (len(dims) - 1 - dim))
    return gain


def profile(count, total, most, lean):
    loads = [(1 << 20) // math.isqrt(standing ** lean) + 1 for standing in range(2, count + 1)]
    spare, counts = total - most - (count - 1), [1] * (count - 1)
    while spare > 0:
        movable = [i for i in range(count - 1) if counts[i] < most]
        whole, remaining = sum([loads[i] for i in movable]), spare
        for i in movable:
            addition = min(most - counts[i], max(1, remaining * loads[i] // whole), spare)
            counts[i] = counts[i] + addition
            spare = spare - addition
    return np.array([most] + counts)


def uneven(rng, number_of, total, bound, slope):
    if number_of == 2:
        one = jax.random.randint(rng, (), max(1, total - bound), min(bound, total - 1) + 1)
        return jnp.stack([one, total - one])
    sizes = jnp.asarray(profile(number_of, total, bound, slope), jnp.int32)
    couples = (number_of - 1) // 2
    giver, taker = sizes[1:1 + 2 * couples:2], sizes[2:2 + 2 * couples:2]
    room = jnp.minimum(giver - 1, bound - taker)
    moved = jax.random.randint(jax.random.fold_in(rng, 1), (couples,), 0, 1 << 20) % (room + 1)
    sizes = sizes.at[1:1 + 2 * couples:2].set(giver - moved).at[2:2 + 2 * couples:2].set(taker + moved)
    return sizes[jax.random.permutation(jax.random.fold_in(rng, 2), number_of)]


def gaussian(key, extent, spread, most, pieces=(), kind=jnp.bfloat16):
    entries = jax.random.normal(key, extent, jnp.float32) * spread
    if len(pieces) > 0:
        entries = steps_of(key, extent, pieces, -0.22, 0.18) * entries
    return jnp.clip(entries, min=-most, max=most).astype(kind)


def setup_inputs(seed: int = 0) -> dict:
    splits = jax.random.split(jax.random.key(seed), 9)
    page_cache = draw_page_cache(jax.random.fold_in(splits[8], 71), 0)
    keep_list = draw_keep_list(jax.random.fold_in(splits[8], 71), 0)
    fold_weight = jnp.clip(jnp.exp(math.log(10.0) - 4.6051702 * jax.random.uniform(splits[2], (PAGES, PSZ), jnp.float32) ** steps_of(splits[2], (PAGES, PSZ), ((0, 8),), -0.2, 0.2)), 0.1, 10.0)
    page_table = draw_page_table(jax.random.fold_in(splits[8], 71), 0)
    lengths = uneven(splits[4], REQS, REQS * MAXP * PSZ * 5 // 8, MAXP * PSZ, 2).astype(jnp.int32)
    queries = draw_queries(jax.random.fold_in(splits[8], 71), 0)
    fresh_entries = gaussian(splits[6], (REQS, 2, KVH, HD), 1.0, 6.0, ((0, 8), (2, 4)))
    out_weight = gaussian(splits[7], (HQ * HD, D), (HQ * HD) ** -0.5, 0.125, ((0, 4),))
    return {"page_cache": page_cache, "keep_list": keep_list, "fold_weight": fold_weight, "page_table": page_table, "lengths": lengths, "queries": queries, "fresh_entries": fresh_entries, "out_weight": out_weight}


negative_floor = -1e30


def compact_page(inputs):
    page, keep_row, weight_row, valid_count = inputs
    slot_index = jnp.arange(PSZ, dtype=jnp.int32)
    valid = slot_index < valid_count
    kept_mask = jnp.logical_and(valid, keep_row > 0)
    dropped = jnp.logical_and(valid, keep_row == 0)
    kept_flag = kept_mask.astype(jnp.int32)
    position = jnp.cumsum(kept_flag) - kept_flag
    total_kept = jnp.sum(kept_flag)
    target = jnp.where(kept_mask, position, PSZ).astype(jnp.int32)
    moved = jnp.zeros_like(page).at[:, :, target, :].set(page, mode="drop")
    dropped_weight = jnp.where(dropped, weight_row, 0.0)
    weight_sum = jnp.sum(dropped_weight)
    folded = jnp.einsum("t,chtd->chd", dropped_weight, page.astype(jnp.float32), precision=lax.Precision.HIGHEST)
    folded = (folded / jnp.maximum(weight_sum, 1.0)).astype(jnp.bfloat16)
    at_fold = slot_index == total_kept
    packed = jnp.where(at_fold[None, None, :, None], folded[:, :, None, :], moved)
    page_mass = jnp.where(slot_index < total_kept, 1.0, jnp.where(at_fold, weight_sum, 0.0)).astype(jnp.bfloat16)
    return packed, page_mass


def reference(page_cache, keep_list, fold_weight, page_table, lengths, queries, fresh_entries, out_weight):
    table_flat = page_table.reshape(-1).astype(jnp.int32)
    logical = jnp.zeros((PAGES,), jnp.int32).at[table_flat].set(jnp.arange(PAGES, dtype=jnp.int32))
    request = logical // MAXP
    within = logical % MAXP
    valid_count = jnp.clip(lengths[request] - within * PSZ, 0, PSZ).astype(jnp.int32)
    packed_cache, packed_mass = lax.map(compact_page, (page_cache, keep_list, fold_weight, valid_count))
    score_scale = HD ** -0.5
    groups = HQ // KVH

    def attend(inputs):
        rows, query_row, fresh = inputs
        pages = packed_cache[rows]
        page_mass = packed_mass[rows].astype(jnp.float32)
        query_f = query_row.astype(jnp.float32).reshape(KVH, groups, HD)
        keys = pages[:, 0].astype(jnp.float32)
        values = pages[:, 1].astype(jnp.float32)
        scores = jnp.einsum("hgd,phtd->phgt", query_f, keys) * score_scale
        live_mask = (page_mass > 0)[:, None, None, :]
        page_top = jnp.max(jnp.where(live_mask, scores, negative_floor), axis=-1)
        weights = jnp.where(live_mask, page_mass[:, None, None, :] * jnp.exp(scores - page_top[..., None]), 0.0)
        page_total = jnp.sum(weights, axis=-1)
        rounded = lax.optimization_barrier(weights.astype(jnp.bfloat16)).astype(jnp.float32)
        page_part = jnp.einsum("phgt,phtd->phgd", rounded, values)
        fresh_key = fresh[0].astype(jnp.float32)
        fresh_value = fresh[1].astype(jnp.float32)
        own_score = jnp.einsum("hgd,hd->hg", query_f, fresh_key) * score_scale
        best_score = jnp.maximum(jnp.max(page_top, axis=0), own_score)
        factor = jnp.exp(page_top - best_score[None])
        own_factor = jnp.exp(own_score - best_score)
        denominator = jnp.sum(factor * page_total, axis=0) + own_factor
        numerator = jnp.sum(factor[..., None] * page_part, axis=0) + own_factor[..., None] * fresh_value[:, None, :]
        return (numerator / denominator[..., None]).astype(jnp.bfloat16).reshape(HQ * HD)

    attended = lax.map(attend, (page_table.astype(jnp.int32), queries, fresh_entries))
    projected = jnp.dot(attended, out_weight, preferred_element_type=jnp.float32).astype(jnp.bfloat16)
    return packed_cache, packed_mass, attended, projected
```

```python
import functools

import jax
import jax.numpy as jnp
from jax import lax
from jax.experimental import pallas as pl
from jax.experimental.pallas import tpu as pltpu
from jax.sharding import PartitionSpec as P

negative_floor = -1e30
f32 = jnp.float32
bf16 = jnp.bfloat16
i32 = jnp.int32


def iota(shape, dim):
    return lax.broadcasted_iota(i32, shape, dim)


def dot(a, b, contract=(1, 0)):
    return lax.dot_general(
        a, b, (((contract[0],), (contract[1],)), ((), ())), preferred_element_type=f32
    )


def pieces(x):
    high = x.astype(bf16)
    rest = x - high.astype(f32)
    middle = rest.astype(bf16)
    low = (rest - middle.astype(f32)).astype(bf16)
    return high, middle, low


def ones_where(mask):
    return jnp.where(mask, 1.0, 0.0).astype(bf16)


def compact_kernel(
    heads, req_dev, base_ref, table_ref, lengths_ref, keep_ref, weight_ref, pages_ref,
    packed_ref, mass_ref, kept_ref, fold_mass_ref, folded_ref, request_ref, slot_ref,
    position_ref, count_ref, share_ref,
):
    step = pl.program_id(0)
    group = pages_ref.shape[0]
    pages_dev, slots = keep_ref.shape
    reqs, max_pages = table_ref.shape

    @pl.when(step == 0)
    def _():
        base = base_ref[0]
        diagonal = iota((reqs, reqs), 0) == iota((reqs, reqs), 1)
        lengths = jnp.sum(
            jnp.where(diagonal, jnp.broadcast_to(lengths_ref[...], (reqs, reqs)), 0),
            axis=1, keepdims=True,
        )
        page_id = iota((reqs, pages_dev), 1) + base
        valid = jnp.zeros((reqs, pages_dev), i32)
        owns = jnp.zeros((reqs, pages_dev), i32)
        for j in range(max_pages):
            match = table_ref[:, j : j + 1] == page_id
            left = jnp.clip(lengths - j * slots, 0, slots)
            valid = valid + jnp.where(match, left, 0)
            owns = owns + jnp.where(match, 1, 0)
        valid_count = dot(valid.astype(f32).astype(bf16), jnp.ones((reqs, slots), bf16), (0, 0))
        owns_f = owns.astype(f32)
        owns_b = owns_f.astype(bf16)
        request = dot(owns_b, iota((reqs, slots), 0).astype(f32).astype(bf16), (0, 0))
        slot_index = iota((pages_dev, slots), 1).astype(f32)
        in_page = slot_index < valid_count
        kept = jnp.logical_and(in_page, keep_ref[...] > 0)
        dropped = jnp.logical_and(in_page, keep_ref[...] == 0)
        kept_f = jnp.where(kept, 1.0, 0.0)
        before = ones_where(iota((slots, slots), 0) < iota((slots, slots), 1))
        position = dot(kept_f.astype(bf16), before)
        count = jnp.sum(kept_f, axis=1, keepdims=True)
        dropped_weight = jnp.where(dropped, weight_ref[...], 0.0)
        weight_sum = jnp.sum(dropped_weight, axis=1, keepdims=True)
        mass = jnp.where(
            slot_index < count, 1.0, jnp.where(slot_index == count, weight_sum, 0.0)
        ).astype(bf16)
        mass_ref[...] = mass
        kept_ref[...] = kept_f
        fold_mass_ref[...] = jnp.broadcast_to(
            weight_sum.astype(bf16).astype(f32), (pages_dev, slots)
        )
        position_ref[...] = jnp.where(kept, position, -1.0)
        count_ref[...] = jnp.broadcast_to(count, (pages_dev, slots))
        share = pieces(dropped_weight / jnp.maximum(weight_sum, 1.0))
        for n in range(3):
            share_ref[n] = share[n].astype(f32)
        rows = pages_dev * heads
        spread = ones_where(iota((rows, pages_dev), 0) // heads == iota((rows, pages_dev), 1))
        request_ref[...] = dot(spread, request.astype(bf16))
        owner_of = (iota((reqs, slots), 0) // req_dev).astype(f32)
        owner_col = dot(owns_b, owner_of.astype(bf16), (0, 0))[:, :pages_dev]
        owner_row = jnp.sum(owns_f * owner_of[:, :pages_dev], axis=0, keepdims=True)
        earlier = jnp.logical_and(
            owner_col == owner_row, iota((pages_dev, pages_dev), 0) < iota((pages_dev, pages_dev), 1)
        )
        rank = jnp.sum(jnp.where(earlier, 1.0, 0.0), axis=0, keepdims=True)
        per_owner = pages_dev // (reqs // req_dev)
        slot = jnp.broadcast_to(owner_row * per_owner + rank, (8, pages_dev)).astype(bf16)
        slot_ref[...] = dot(slot, spread, (1, 1))

    row = iota((slots, slots), 0).astype(f32)
    tile_row = iota((16, slots), 0)
    for i in range(group):
        page = step * group + i
        selector = ones_where(row == position_ref[pl.ds(page, 1), :])
        shares = jnp.zeros((16, slots), f32)
        for n in range(3):
            shares = jnp.where(tile_row == n, share_ref[n, pl.ds(page, 1), :], shares)
        left = jnp.concatenate([selector, shares.astype(bf16)], axis=0)
        at_fold = row == count_ref[pl.ds(page, 1), :]
        for c in range(2):
            kv_local = pages_ref.shape[2]
            right = jnp.concatenate([pages_ref[i, c, g] for g in range(kv_local)], axis=1)
            result = dot(left, right)
            folded = jnp.sum(result[slots : slots + 8], axis=0, keepdims=True)
            folded = folded.astype(bf16).astype(f32)
            for g in range(kv_local):
                part = slice(g * 128, (g + 1) * 128)
                folded_ref[c, g, pl.ds(page, 1), :] = folded[:, part]
                packed_ref[i, c, g] = jnp.where(
                    at_fold, folded[:, part], result[:slots, part]
                ).astype(bf16)


def compact(base, page_table, lengths, keep_list, fold_weight, page_cache, heads, req_dev, group):
    pages_dev, _, kv_local, slots, head_size = page_cache.shape
    rows = pages_dev * heads
    whole = lambda *shape: pl.BlockSpec(shape, lambda s: (0,) * len(shape))
    paged = pl.BlockSpec((group, 2, kv_local, slots, head_size), lambda s: (s, 0, 0, 0, 0))
    small = (pages_dev, slots)
    fold = (2, kv_local, pages_dev, head_size)
    return pl.pallas_call(
        functools.partial(compact_kernel, heads, req_dev),
        grid=(pages_dev // group,),
        in_specs=[
            pl.BlockSpec(memory_space=pltpu.SMEM),
            whole(*page_table.shape),
            whole(1, lengths.shape[0]),
            whole(*small),
            whole(*small),
            paged,
        ],
        out_specs=[
            paged, whole(*small), whole(*small), whole(*small), whole(*fold),
            whole(rows, slots), whole(8, rows),
        ],
        out_shape=[
            jax.ShapeDtypeStruct(page_cache.shape, bf16),
            jax.ShapeDtypeStruct(small, bf16),
            jax.ShapeDtypeStruct(small, f32),
            jax.ShapeDtypeStruct(small, f32),
            jax.ShapeDtypeStruct(fold, f32),
            jax.ShapeDtypeStruct((rows, slots), f32),
            jax.ShapeDtypeStruct((8, rows), f32),
        ],
        scratch_shapes=[
            pltpu.VMEM(small, f32),
            pltpu.VMEM(small, f32),
            pltpu.VMEM((3,) + small, f32),
        ],
        compiler_params=pltpu.CompilerParams(vmem_limit_bytes=40 << 20),
        cost_estimate=pl.CostEstimate(
            flops=2 * pages_dev * slots * slots * 2 * kv_local * head_size,
            bytes_accessed=4 * page_cache.size, transcendentals=0,
        ),
        name="compact",
    )(base, page_table, lengths.reshape(1, -1), keep_list, fold_weight, page_cache)


def attend_kernel(
    heads, score_scale, chunk, query_ref, kept_ref, fold_mass_ref, folded_ref, request_ref, slot_ref,
    pages_ref, out_ref, keys, values, scores, parts, key_sem, value_sem,
):
    pages_dev, slots = kept_ref.shape
    kv_local = folded_ref.shape[1]
    groups = heads // kv_local
    rows = pages_dev * heads
    copies = []
    for c, (buffer, sem) in enumerate(((keys, key_sem), (values, value_sem))):
        for n in range(pages_dev // chunk):
            span = pl.ds(n * chunk, chunk)
            copies.append(
                pltpu.make_async_copy(pages_ref.at[span, c], buffer.at[span], sem.at[n])
            )
    for copy in copies:
        copy.start()
    key_copies, value_copies = copies[: len(copies) // 2], copies[len(copies) // 2 :]

    all_rows = query_ref.shape[0]
    target = request_ref[...] * heads + (iota((rows, slots), 0) % heads).astype(f32)
    query = jnp.zeros((rows, 128), f32)
    for n in range(all_rows // slots):
        pick = ones_where(target == (iota((rows, slots), 1) + n * slots).astype(f32))
        query = query + dot(pick, query_ref[n * slots : (n + 1) * slots])
    query_b = query.astype(bf16)

    tile = 16
    tile_pages = tile // heads
    row = iota((tile, 128), 0)
    row_page = row // heads
    row_group = (row % heads) // groups

    def choose(results):
        chosen = None
        for i in range(tile_pages):
            for g in range(kv_local):
                piece = results[i][:, g * 128 : (g + 1) * 128]
                if chosen is None:
                    chosen = piece
                else:
                    here = jnp.logical_and(row_page == i, row_group == g)
                    chosen = jnp.where(here, piece, chosen)
        return chosen

    for n in range(pages_dev // chunk):
        key_copies[n].wait()
        for m in range(chunk // tile_pages):
            first = n * chunk + m * tile_pages
            at = first * heads
            left = query_b[at : at + tile]
            results = [
                dot(left, keys[first + i].reshape(kv_local * slots, 128), (1, 1))
                for i in range(tile_pages)
            ]
            scores[at : at + tile, :] = choose(results)

    spread = ones_where(iota((rows, pages_dev), 0) // heads == iota((rows, pages_dev), 1))
    group_of = (iota((rows, pages_dev), 0) % heads) // groups
    kept = dot(spread, kept_ref[...].astype(bf16)) > 0.5
    fold_mass = dot(spread, fold_mass_ref[...].astype(bf16))[:, :1]
    fold_key = jnp.zeros((rows, 128), f32)
    fold_value = jnp.zeros((rows, 128), f32)
    for g in range(kv_local):
        spread_g = jnp.where(group_of == g, spread.astype(f32), 0.0).astype(bf16)
        fold_key = fold_key + dot(spread_g, folded_ref[0, g].astype(bf16))
        fold_value = fold_value + dot(spread_g, folded_ref[1, g].astype(bf16))
    fold_score = jnp.sum(query * fold_key, axis=1, keepdims=True) * score_scale
    fold_live = fold_mass > 0
    score = jnp.where(kept, scores[...] * score_scale, negative_floor)
    top = jnp.maximum(
        jnp.max(score, axis=1, keepdims=True), jnp.where(fold_live, fold_score, negative_floor)
    )
    weight = jnp.where(kept, jnp.exp(score - top), 0.0)
    fold_weight = jnp.where(fold_live, fold_mass * jnp.exp(fold_score - top), 0.0)
    total = jnp.sum(weight, axis=1, keepdims=True) + fold_weight
    weight_b = weight.astype(bf16)

    for n in range(pages_dev // chunk):
        value_copies[n].wait()
        for m in range(chunk // tile_pages):
            first = n * chunk + m * tile_pages
            at = first * heads
            left = weight_b[at : at + tile]
            results = [
                dot(left, jnp.concatenate([values[first + i, g] for g in range(kv_local)], axis=1))
                for i in range(tile_pages)
            ]
            parts[at : at + tile, :] = choose(results)

    part = parts[...] + fold_weight.astype(bf16).astype(f32) * fold_value
    lane = iota((rows, 128), 1)
    stats = jnp.where(lane == 6, request_ref[...], 0.0)
    for n, piece in enumerate(pieces(top) + pieces(total)):
        stats = jnp.where(lane == n, piece.astype(f32), stats)
    send = jnp.concatenate([part.astype(bf16), stats.astype(bf16)], axis=1)
    place = slot_ref[:1] * heads + (iota((1, rows), 1) % heads).astype(f32)
    move = ones_where(iota((rows, rows), 0).astype(f32) == place)
    out_ref[...] = dot(move, send).astype(bf16)


def attend(queries, kept, fold_mass, folded, request, slot, page_cache, score_scale, heads):
    pages_dev, _, kv_local, slots, head_size = page_cache.shape
    rows = pages_dev * heads
    chunk = 8
    vmem = pl.BlockSpec(memory_space=pltpu.VMEM)
    return pl.pallas_call(
        functools.partial(attend_kernel, heads, score_scale, chunk),
        in_specs=[vmem] * 6 + [pl.BlockSpec(memory_space=pl.ANY)],
        out_specs=vmem,
        out_shape=jax.ShapeDtypeStruct((rows, 2 * head_size), bf16),
        scratch_shapes=[
            pltpu.VMEM((pages_dev, kv_local, slots, head_size), bf16),
            pltpu.VMEM((pages_dev, kv_local, slots, head_size), bf16),
            pltpu.VMEM((rows, slots), f32),
            pltpu.VMEM((rows, head_size), f32),
            pltpu.SemaphoreType.DMA((pages_dev // chunk,)),
            pltpu.SemaphoreType.DMA((pages_dev // chunk,)),
        ],
        compiler_params=pltpu.CompilerParams(vmem_limit_bytes=40 << 20),
        cost_estimate=pl.CostEstimate(
            flops=4 * rows * slots * head_size * 16, bytes_accessed=2 * page_cache.size,
            transcendentals=rows * slots,
        ),
        name="attend",
    )(queries, kept, fold_mass, folded, request, slot, page_cache)


def combine_kernel(
    heads, req_dev, score_scale, kv_count, first_ref, rank_ref, got_ref, query_ref, fresh_key_ref,
    fresh_value_ref, weight_ref, attended_ref, *out_refs
):
    rows = got_ref.shape[0]
    cols = heads * req_dev
    width = weight_ref.shape[1] // kv_count
    stats = got_ref[:, 128:].astype(f32)
    top = stats[:, 0:1] + stats[:, 1:2] + stats[:, 2:3]
    request = stats[:, 6:7] - first_ref[0].astype(f32)
    row_head = (iota((rows, cols), 0) % heads).astype(f32)
    col = iota((rows, cols), 1)
    match = jnp.logical_and(
        request == (col % req_dev).astype(f32), row_head == (col // req_dev).astype(f32)
    )
    own = jnp.sum(
        query_ref[...].astype(f32) * fresh_key_ref[...].astype(f32), axis=1, keepdims=True
    ) * score_scale
    diagonal = iota((cols, cols), 0) == iota((cols, cols), 1)
    own_row = jnp.sum(jnp.where(diagonal, own, 0.0), axis=0, keepdims=True)
    best = jnp.maximum(
        jnp.max(jnp.where(match, top, negative_floor), axis=0, keepdims=True), own_row
    )
    best_col = jnp.sum(jnp.where(diagonal, best, 0.0), axis=1, keepdims=True)
    factor = jnp.where(match, jnp.exp(top - best), 0.0)
    high, middle, low = pieces(factor)
    got = got_ref[...]
    sums = dot(high, got, (0, 0)) + dot(middle, got, (0, 0)) + dot(low, got, (0, 0))
    own_factor = jnp.exp(own - best_col)
    denominator = sums[:, 131:132] + sums[:, 132:133] + sums[:, 133:134] + own_factor
    numerator = sums[:, :128] + own_factor * fresh_value_ref[...].astype(f32)
    attended = numerator / denominator
    attended = jnp.concatenate(
        [attended[h * req_dev : (h + 1) * req_dev] for h in range(heads)], axis=1
    ).astype(bf16)
    attended_ref[...] = attended
    rank = rank_ref[0]
    for k in range(kv_count):
        other = lax.rem(rank + k, kv_count)
        at = pl.multiple_of(other * width, width)
        out_refs[k][...] = dot(attended, weight_ref[:, pl.ds(at, width)]).astype(bf16)


def combine(first, rank, got, query, fresh_key, fresh_value, out_weight, score_scale, heads, kv_count):
    req_dev = query.shape[0] // heads
    vmem = pl.BlockSpec(memory_space=pltpu.VMEM)
    smem = pl.BlockSpec(memory_space=pltpu.SMEM)
    width = out_weight.shape[1] // kv_count
    return pl.pallas_call(
        functools.partial(combine_kernel, heads, req_dev, score_scale, kv_count),
        in_specs=[smem, smem] + [vmem] * 5,
        out_specs=[vmem] * (1 + kv_count),
        out_shape=[jax.ShapeDtypeStruct((req_dev, out_weight.shape[0]), bf16)]
        + [jax.ShapeDtypeStruct((req_dev, width), bf16)] * kv_count,
        compiler_params=pltpu.CompilerParams(vmem_limit_bytes=40 << 20),
        cost_estimate=pl.CostEstimate(
            flops=2 * req_dev * out_weight.size, bytes_accessed=2 * out_weight.size, transcendentals=0
        ),
        name="combine",
    )(first, rank, got, query, fresh_key, fresh_value, out_weight)


def per_device(
    page_cache, keep_list, fold_weight, page_table, lengths, queries, fresh_entries, out_weight
):
    seq_count = lax.axis_size("seq")
    kv_count = lax.axis_size("kv")
    seq_rank = lax.axis_index("seq").astype(i32).reshape(1)
    kv_rank = lax.axis_index("kv").astype(i32).reshape(1)
    pages_dev, _, kv_local, slots, head_size = page_cache.shape
    req_dev, heads, _ = queries.shape
    groups = heads // kv_local
    score_scale = head_size ** (-0.5)

    rows = queries.reshape(req_dev * heads, head_size)
    query_all = lax.all_to_all(
        jnp.broadcast_to(rows[None], (seq_count,) + rows.shape), "seq",
        split_axis=0, concat_axis=0, tiled=True,
    ).reshape(seq_count * req_dev * heads, head_size)
    packed, mass, kept, fold_mass, folded, request, slot = compact(
        seq_rank * pages_dev, page_table, lengths, keep_list, fold_weight, page_cache,
        heads, req_dev, 4,
    )
    send = attend(
        query_all, kept, fold_mass, folded, request, slot, page_cache, score_scale, heads
    )
    got = lax.all_to_all(
        send.reshape(seq_count, -1, send.shape[1]), "seq", split_axis=0, concat_axis=0, tiled=True
    ).reshape(send.shape)
    by_head = lambda x: x.transpose(1, 0, 2).reshape(heads * req_dev, head_size)
    fresh = jnp.repeat(fresh_entries, groups, axis=2)
    attended, *shares = combine(
        seq_rank * req_dev, kv_rank, got, by_head(queries), by_head(fresh[:, 0]),
        by_head(fresh[:, 1]), out_weight, score_scale, heads, kv_count,
    )
    total = shares[0].astype(f32)
    for k in range(1, kv_count):
        moved = lax.ppermute(shares[k], "kv", [(i, (i + k) % kv_count) for i in range(kv_count)])
        total = total + moved.astype(f32)
    return packed, mass, attended, total.astype(bf16)


def solution(mesh):
    placed = (
        P("seq", None, "kv", None, None),
        P("seq", None),
        P("seq", None),
        P(),
        P(),
        P("seq", "kv", None),
        P("seq", None, "kv", None),
        P("kv", None),
    )
    return jax.shard_map(
        per_device,
        mesh=mesh,
        in_specs=placed,
        out_specs=(
            P("seq", None, "kv", None, None),
            P("seq", None),
            P("seq", "kv"),
            P("seq", "kv"),
        ),
        check_vma=False,
    )
```

```python
import functools

import jax
import jax.numpy as jnp
from jax import lax
from jax.experimental import pallas as pl
from jax.experimental.pallas import tpu as pltpu
from jax.sharding import PartitionSpec as P

negative_floor = -1e30
f32 = jnp.float32
bf16 = jnp.bfloat16
i32 = jnp.int32


def iota(shape, dim):
    return lax.broadcasted_iota(i32, shape, dim)


def dot(a, b, contract=(1, 0)):
    return lax.dot_general(
        a, b, (((contract[0],), (contract[1],)), ((), ())), preferred_element_type=f32
    )


def pieces(x):
    high = x.astype(bf16)
    rest = x - high.astype(f32)
    middle = rest.astype(bf16)
    low = (rest - middle.astype(f32)).astype(bf16)
    return high, middle, low


def ones_where(mask):
    return jnp.where(mask, 1.0, 0.0).astype(bf16)


def spread_rows(pages_dev, heads):
    rows = pages_dev * heads
    return ones_where(iota((rows, pages_dev), 0) // heads == iota((rows, pages_dev), 1))


def select_left(page, position, count_ref, slots):
    row = iota((slots, slots), 0).astype(f32)
    selector = ones_where(row == position[pl.ds(page, 1), :])
    return selector, row == count_ref[pl.ds(page, 1), :]


def share_rows(page, share):
    row = iota((16, share.shape[2]), 0)
    rows = jnp.zeros((16, share.shape[2]), f32)
    for n in range(3):
        rows = jnp.where(row == n, share[n, pl.ds(page, 1), :], rows)
    return rows.astype(bf16)


def rounded_fold(rows):
    return jnp.sum(rows, axis=0, keepdims=True).astype(bf16).astype(f32)


def side_by_side(ref, page):
    return jnp.concatenate([ref[page, g] for g in range(ref.shape[1])], axis=1)


def prepare_kernel(
    heads, req_dev, chunk, rank_ref, table_hbm, lengths_hbm, keep_hbm, weight_hbm, query_hbm,
    pages_hbm, keys, query_ref, mass_ref, kept_ref, fold_mass_ref, position_ref, count_ref, share_ref,
    folded_ref, target_ref, slot_ref,
    table_ref, lengths_ref, keep_ref, weight_ref, small_sem, in_sem,
):
    pages_dev, slots = keep_ref.shape
    max_pages, reqs = table_ref.shape
    kv_local = keys.shape[1]
    chunks = pages_dev // chunk
    small = [
        pltpu.make_async_copy(a, b, small_sem.at[n])
        for n, (a, b) in enumerate(
            ((table_hbm, table_ref), (lengths_hbm, lengths_ref), (keep_hbm, keep_ref),
             (weight_hbm, weight_ref), (query_hbm, query_ref))
        )
    ]
    for copy in small:
        copy.start()
    loads = [
        pltpu.make_async_copy(
            pages_hbm.at[pl.ds(n * chunk, chunk), 0], keys.at[pl.ds(n * chunk, chunk)], in_sem.at[n]
        )
        for n in range(chunks)
    ]
    for copy in loads:
        copy.start()
    for copy in small:
        copy.wait()

    rank = rank_ref[0]
    page_id = iota((pages_dev, reqs), 0) + rank * pages_dev
    req_id = iota((pages_dev, reqs), 1)
    valid = jnp.zeros((pages_dev, reqs), i32)
    request = jnp.zeros((pages_dev, reqs), i32)
    for j in range(max_pages):
        match = table_ref[j : j + 1, :] == page_id
        left = jnp.clip(lengths_ref[...] - j * slots, 0, slots)
        valid = valid + jnp.where(match, left, 0)
        request = request + jnp.where(match, req_id, 0)
    valid = jnp.sum(valid, axis=1, keepdims=True)
    request = jnp.sum(request, axis=1, keepdims=True)
    slot_index = iota((pages_dev, slots), 1)
    in_page = slot_index < valid
    kept = jnp.logical_and(in_page, keep_ref[...] > 0)
    dropped = jnp.logical_and(in_page, keep_ref[...] == 0)
    kept_f = jnp.where(kept, 1.0, 0.0)
    before = ones_where(iota((slots, slots), 0) < iota((slots, slots), 1))
    position = dot(kept_f.astype(bf16), before)
    count = jnp.sum(kept_f, axis=1, keepdims=True)
    dropped_weight = jnp.where(dropped, weight_ref[...], 0.0)
    weight_sum = jnp.sum(dropped_weight, axis=1, keepdims=True)
    slot_f = slot_index.astype(f32)
    mass_ref[...] = jnp.where(
        slot_f < count, 1.0, jnp.where(slot_f == count, weight_sum, 0.0)
    ).astype(bf16)
    kept_ref[...] = kept_f
    fold_mass_ref[...] = jnp.broadcast_to(weight_sum.astype(bf16).astype(f32), (pages_dev, slots))
    position_ref[...] = jnp.where(kept, position, -1.0)
    count_ref[...] = jnp.broadcast_to(count, (pages_dev, slots))
    share = pieces(dropped_weight / jnp.maximum(weight_sum, 1.0))
    for n in range(3):
        share_ref[n] = share[n].astype(f32)

    owner = request // req_dev
    chip, core = owner // 2, owner % 2
    from_chip = jnp.bitwise_xor(chip, rank // 2)
    from_core = jnp.where(core == rank % 2, 0, 1)
    at_hand = (from_core * (reqs // req_dev // 2) + from_chip) * req_dev + request % req_dev
    at_hand = jnp.broadcast_to(at_hand, (pages_dev, slots)).astype(f32)
    spread = spread_rows(pages_dev, heads)
    rows = pages_dev * heads
    target_ref[...] = dot(spread, at_hand.astype(bf16)).astype(i32) * heads + iota((rows, slots), 0) % heads
    owner_col = jnp.broadcast_to(owner, (pages_dev, pages_dev))
    page_row, page_col = iota((pages_dev, pages_dev), 0), iota((pages_dev, pages_dev), 1)
    owner_row = jnp.sum(jnp.where(page_row == page_col, owner_col, 0), axis=0, keepdims=True)
    earlier = jnp.logical_and(owner_col == owner_row, page_row < page_col)
    order = jnp.sum(jnp.where(earlier, 1, 0), axis=0, keepdims=True)
    slot = owner_row * (pages_dev // (reqs // req_dev)) + order
    slot = jnp.broadcast_to(slot, (8, pages_dev)).astype(f32).astype(bf16)
    slot_ref[...] = dot(slot, spread, (1, 1))

    for n in range(chunks):
        loads[n].wait()
        for page in range(n * chunk, (n + 1) * chunk):
            result = dot(share_rows(page, share_ref), side_by_side(keys, page))
            folded = rounded_fold(result[:8])
            for g in range(kv_local):
                folded_ref[g, page : page + 1, :] = folded[:, g * 128 : (g + 1) * 128]


def prepare(rank, page_table, lengths, keep_list, fold_weight, queries, page_cache, heads, req_dev, chunk=16):
    pages_dev, _, kv_local, slots, head_size = page_cache.shape
    reqs, max_pages = page_table.shape
    rows = pages_dev * heads
    chunks = pages_dev // chunk
    hbm = pl.BlockSpec(memory_space=pltpu.HBM)
    vmem = pl.BlockSpec(memory_space=pltpu.VMEM)
    small = (pages_dev, slots)
    return pl.pallas_call(
        functools.partial(prepare_kernel, heads, req_dev, chunk),
        in_specs=[pl.BlockSpec(memory_space=pltpu.SMEM)] + [hbm] * 6,
        out_specs=[vmem] * 11,
        out_shape=[
            pltpu.VMEM((pages_dev, kv_local, slots, head_size), bf16),
            pltpu.VMEM(queries.shape, bf16),
            jax.ShapeDtypeStruct(small, bf16),
            jax.ShapeDtypeStruct(small, f32),
            jax.ShapeDtypeStruct(small, f32),
            jax.ShapeDtypeStruct(small, f32),
            jax.ShapeDtypeStruct(small, f32),
            jax.ShapeDtypeStruct((3,) + small, f32),
            jax.ShapeDtypeStruct((kv_local, pages_dev, head_size), f32),
            jax.ShapeDtypeStruct((rows, slots), i32),
            jax.ShapeDtypeStruct((8, rows), f32),
        ],
        scratch_shapes=[
            pltpu.VMEM((max_pages, reqs), i32),
            pltpu.VMEM((1, reqs), i32),
            pltpu.VMEM(small, i32),
            pltpu.VMEM(small, f32),
            pltpu.SemaphoreType.DMA((5,)),
            pltpu.SemaphoreType.DMA((chunks,)),
        ],
        compiler_params=pltpu.CompilerParams(vmem_limit_bytes=24 << 20),
        name="prepare",
    )(
        rank, *(
            pltpu.with_memory_space_constraint(x, pltpu.HBM)
            for x in (
                page_table.T, lengths.reshape(1, -1), keep_list, fold_weight, queries, page_cache
            )
        )
    )


def pack_kernel(half, chunk, *refs):
    pages_hbm, position_ref, count_ref, folded_ref = refs[:4]
    packed_hbm, raw, staged, in_sem, out_sem = refs[-5:]
    pages_dev, slots = position_ref.shape
    kv_local = raw.shape[1]
    spans = [pl.ds(n * chunk, chunk) for n in range(pages_dev // chunk)]
    loads = [
        pltpu.make_async_copy(pages_hbm.at[span, half], raw.at[span], in_sem.at[n])
        for n, span in enumerate(spans)
    ]
    stores = [
        pltpu.make_async_copy(staged.at[span], packed_hbm.at[span, half], out_sem.at[n])
        for n, span in enumerate(spans)
    ]
    for copy in loads:
        copy.start()
    for n in range(pages_dev // chunk):
        loads[n].wait()
        for page in range(n * chunk, (n + 1) * chunk):
            selector, at_fold = select_left(page, position_ref, count_ref, slots)
            result = dot(selector, side_by_side(raw, page))
            for g in range(kv_local):
                staged[page, g] = jnp.where(
                    at_fold, folded_ref[g, pl.ds(page, 1), :], result[:, g * 128 : (g + 1) * 128]
                ).astype(bf16)
        stores[n].start()
    for copy in stores:
        copy.wait()


def pack(half, page_cache, position, count, folded, packed=None, chunk=8):
    pages_dev, _, kv_local, slots, head_size = page_cache.shape
    hbm = pl.BlockSpec(memory_space=pltpu.HBM)
    vmem = pl.BlockSpec(memory_space=pltpu.VMEM)
    there = [] if packed is None else [packed]
    buffer = pltpu.VMEM((pages_dev, kv_local, slots, head_size), bf16)
    chunks = pltpu.SemaphoreType.DMA((pages_dev // chunk,))
    in_hbm = lambda x: pltpu.with_memory_space_constraint(x, pltpu.HBM)
    return pl.pallas_call(
        functools.partial(pack_kernel, half, chunk),
        in_specs=[hbm] + [vmem] * 3 + [hbm] * len(there),
        out_specs=hbm,
        out_shape=jax.ShapeDtypeStruct(page_cache.shape, bf16),
        input_output_aliases={4: 0} if there else {},
        scratch_shapes=[buffer, buffer, chunks, chunks],
        compiler_params=pltpu.CompilerParams(vmem_limit_bytes=24 << 20),
        name=("pack_keys", "pack_values")[half],
    )(in_hbm(page_cache), position, count, folded, *map(in_hbm, there))


def attend_kernel(
    heads, req_dev, score_scale, chunk, near_ref, far_ref, keys, kept_ref, fold_mass_ref, share_ref,
    fold_key_ref, target_ref, slot_ref, pages_hbm, out_ref, fold_value_ref, scores, parts, values,
    value_sem,
):
    pages_dev, slots = kept_ref.shape
    kv_local = keys.shape[1]
    loads = [
        pltpu.make_async_copy(
            pages_hbm.at[pl.ds(n * chunk, chunk), 1], values.at[pl.ds(n * chunk, chunk)],
            value_sem.at[n],
        )
        for n in range(pages_dev // chunk)
    ]
    for copy in loads:
        copy.start()
    groups = heads // kv_local
    rows = pages_dev * heads
    spread = spread_rows(pages_dev, heads)

    half = near_ref.shape[0]
    query = jnp.zeros((rows, 128), f32)
    for n, ref in enumerate((near_ref, far_ref)):
        for m in range(half // slots):
            first = n * half + m * slots
            pick = ones_where(target_ref[...] == iota((rows, slots), 1) + first)
            query = query + dot(pick, ref[m * slots : (m + 1) * slots])
    query_b = query.astype(bf16)

    tile = 16
    tile_pages = tile // heads
    row = iota((tile, 128), 0)
    row_page = row // heads
    row_group = (row % heads) // groups

    def choose(results):
        chosen = results[0][:tile, :128]
        for i in range(tile_pages):
            for g in range(kv_local):
                if i + g > 0:
                    here = jnp.logical_and(row_page == i, row_group == g)
                    chosen = jnp.where(here, results[i][:tile, g * 128 : (g + 1) * 128], chosen)
        return chosen

    for first in range(0, pages_dev, tile_pages):
        at = first * heads
        left = query_b[at : at + tile]
        results = [
            dot(left, keys[first + i].reshape(kv_local * slots, 128), (1, 1))
            for i in range(tile_pages)
        ]
        scores[at : at + tile, :] = choose(results)

    group_of = (iota((rows, pages_dev), 0) % heads) // groups
    spread_g = [
        jnp.where(group_of == g, spread.astype(f32), 0.0).astype(bf16) for g in range(kv_local)
    ]

    def spread_fold(ref):
        return sum(dot(spread_g[g], ref[g].astype(bf16)) for g in range(kv_local))

    kept = dot(spread, kept_ref[...].astype(bf16)) > 0.5
    fold_mass = dot(spread, fold_mass_ref[...].astype(bf16))[:, :1]
    fold_score = jnp.sum(query * spread_fold(fold_key_ref), axis=1, keepdims=True) * score_scale
    fold_live = fold_mass > 0
    score = jnp.where(kept, scores[...] * score_scale, negative_floor)
    top = jnp.maximum(
        jnp.max(score, axis=1, keepdims=True), jnp.where(fold_live, fold_score, negative_floor)
    )
    weight = jnp.where(kept, jnp.exp(score - top), 0.0)
    fold_weight = jnp.where(fold_live, fold_mass * jnp.exp(fold_score - top), 0.0)
    total = jnp.sum(weight, axis=1, keepdims=True) + fold_weight
    weight_b = weight.astype(bf16)

    for first in range(0, pages_dev, tile_pages):
        if first % chunk == 0:
            loads[first // chunk].wait()
        at = first * heads
        results = []
        for i in range(tile_pages):
            left = jnp.concatenate(
                [weight_b[at : at + tile], share_rows(first + i, share_ref)], axis=0
            )
            result = dot(left, side_by_side(values, first + i))
            results.append(result)
            folded = rounded_fold(result[tile : tile + 8])
            for g in range(kv_local):
                fold_value_ref[g, first + i : first + i + 1, :] = folded[:, g * 128 : (g + 1) * 128]
        parts[at : at + tile, :] = choose(results)

    part = parts[...] + fold_weight.astype(bf16).astype(f32) * spread_fold(fold_value_ref)
    lane = iota((rows, 128), 1)
    local = (target_ref[...] // heads % req_dev).astype(f32)
    stats = jnp.where(lane == 6, local, 0.0)
    for n, piece in enumerate(pieces(top) + pieces(total)):
        stats = jnp.where(lane == n, piece.astype(f32), stats)
    send = jnp.concatenate([part.astype(bf16), stats.astype(bf16)], axis=1)
    place = slot_ref[:1] * heads + (iota((1, rows), 1) % heads).astype(f32)
    move = ones_where(iota((rows, rows), 0).astype(f32) == place)
    out_ref[...] = dot(move, send).astype(bf16)


def attend(
    near, far, keys, kept, fold_mass, share, fold_key, target, slot, page_cache, score_scale, heads,
    req_dev, chunk=16
):
    pages_dev, _, kv_local, slots, head_size = page_cache.shape
    rows = pages_dev * heads
    vmem = pl.BlockSpec(memory_space=pltpu.VMEM)
    return pl.pallas_call(
        functools.partial(attend_kernel, heads, req_dev, score_scale, chunk),
        in_specs=[vmem] * 9 + [pl.BlockSpec(memory_space=pltpu.HBM)],
        out_specs=[vmem] * 2,
        out_shape=[
            jax.ShapeDtypeStruct((rows, 2 * head_size), bf16),
            jax.ShapeDtypeStruct((kv_local, pages_dev, head_size), f32),
        ],
        scratch_shapes=[
            pltpu.VMEM((rows, slots), f32),
            pltpu.VMEM((rows, head_size), f32),
            pltpu.VMEM((pages_dev, kv_local, slots, head_size), bf16),
            pltpu.SemaphoreType.DMA((pages_dev // chunk,)),
        ],
        compiler_params=pltpu.CompilerParams(vmem_limit_bytes=24 << 20),
        name="attend",
    )(
        near, far, keys, kept, fold_mass, share, fold_key, target, slot,
        pltpu.with_memory_space_constraint(page_cache, pltpu.HBM),
    )


def combine_kernel(
    heads, req_dev, score_scale, kv_count, rank_ref, got_ref, query_ref, fresh_key_ref,
    fresh_value_ref, weight_ref, attended_ref, *out_refs
):
    rows = got_ref.shape[0]
    cols = heads * req_dev
    width = weight_ref.shape[1] // kv_count
    stats = got_ref[:, 128:].astype(f32)
    top = stats[:, 0:1] + stats[:, 1:2] + stats[:, 2:3]
    request = stats[:, 6:7]
    row_head = (iota((rows, cols), 0) % heads).astype(f32)
    col = iota((rows, cols), 1)
    match = jnp.logical_and(
        request == (col % req_dev).astype(f32), row_head == (col // req_dev).astype(f32)
    )
    own = jnp.sum(
        query_ref[...].astype(f32) * fresh_key_ref[...].astype(f32), axis=1, keepdims=True
    ) * score_scale
    diagonal = iota((cols, cols), 0) == iota((cols, cols), 1)
    own_row = jnp.sum(jnp.where(diagonal, own, 0.0), axis=0, keepdims=True)
    best = jnp.maximum(
        jnp.max(jnp.where(match, top, negative_floor), axis=0, keepdims=True), own_row
    )
    best_col = jnp.sum(jnp.where(diagonal, best, 0.0), axis=1, keepdims=True)
    factor = jnp.where(match, jnp.exp(top - best), 0.0)
    high, middle, low = pieces(factor)
    got = got_ref[...]
    sums = dot(high, got, (0, 0)) + dot(middle, got, (0, 0)) + dot(low, got, (0, 0))
    own_factor = jnp.exp(own - best_col)
    denominator = sums[:, 131:132] + sums[:, 132:133] + sums[:, 133:134] + own_factor
    numerator = sums[:, :128] + own_factor * fresh_value_ref[...].astype(f32)
    attended = numerator / denominator
    attended = jnp.concatenate(
        [attended[h * req_dev : (h + 1) * req_dev] for h in range(heads)], axis=1
    ).astype(bf16)
    attended_ref[...] = attended
    rank = rank_ref[0]
    for k in range(kv_count):
        other = jnp.bitwise_xor(rank, k)
        at = pl.multiple_of(other * width, width)
        out_refs[k][...] = dot(attended, weight_ref[:, pl.ds(at, width)]).astype(bf16)


def combine(rank, got, query, fresh_key, fresh_value, out_weight, score_scale, heads, kv_count):
    req_dev = query.shape[0] // heads
    vmem = pl.BlockSpec(memory_space=pltpu.VMEM)
    smem = pl.BlockSpec(memory_space=pltpu.SMEM)
    width = out_weight.shape[1] // kv_count
    return pl.pallas_call(
        functools.partial(combine_kernel, heads, req_dev, score_scale, kv_count),
        in_specs=[smem] + [vmem] * 5,
        out_specs=[vmem] * (1 + kv_count),
        out_shape=[jax.ShapeDtypeStruct((req_dev, out_weight.shape[0]), bf16)]
        + [jax.ShapeDtypeStruct((req_dev, width), bf16)] * kv_count,
        compiler_params=pltpu.CompilerParams(vmem_limit_bytes=24 << 20),
        cost_estimate=pl.CostEstimate(
            flops=2 * req_dev * out_weight.size, bytes_accessed=2 * out_weight.size, transcendentals=0
        ),
        name="combine",
    )(rank, got, query, fresh_key, fresh_value, out_weight)


def exchange(x, axis, count, mask):
    return lax.ppermute(x, axis, [(i, i ^ mask) for i in range(count)])


def per_device(
    page_cache, keep_list, fold_weight, page_table, lengths, queries, fresh_entries, out_weight
):
    seq_count = lax.axis_size("seq")
    kv_count = lax.axis_size("kv")
    assert seq_count & (seq_count - 1) == 0 and kv_count & (kv_count - 1) == 0
    seq_rank = lax.axis_index("seq").astype(i32).reshape(1)
    kv_rank = lax.axis_index("kv").astype(i32).reshape(1)
    _, _, kv_local, slots, head_size = page_cache.shape
    req_dev, heads, _ = queries.shape
    groups = heads // kv_local
    score_scale = head_size ** (-0.5)

    others = [exchange(queries, "seq", seq_count, 2 * k) for k in range(1, seq_count // 2)]
    keys, own, mass, kept, fold_mass, position, count, share, fold_key, target, slot = prepare(
        seq_rank, page_table, lengths, keep_list, fold_weight, queries, page_cache, heads, req_dev
    )
    near = jnp.concatenate([own] + others, axis=0).reshape(-1, head_size)
    far = exchange(near, "seq", seq_count, 1)
    send, fold_value = attend(
        near, far, keys, kept, fold_mass, share, fold_key, target, slot, page_cache, score_scale,
        heads, req_dev,
    )
    got = lax.all_to_all(
        send.reshape(seq_count, -1, send.shape[1]), "seq", split_axis=0, concat_axis=0, tiled=True
    ).reshape(send.shape)
    packed = pack(1, page_cache, position, count, fold_value)
    got, packed = lax.optimization_barrier((got, packed))
    by_head = lambda x: x.transpose(1, 0, 2).reshape(heads * req_dev, head_size)
    fresh = jnp.repeat(fresh_entries, groups, axis=2)
    attended, *shares = combine(
        kv_rank, got, by_head(queries), by_head(fresh[:, 0]), by_head(fresh[:, 1]), out_weight,
        score_scale, heads, kv_count,
    )
    fold_key, *shares = lax.optimization_barrier((fold_key, *shares))
    total = shares[0].astype(f32)
    for k in range(1, kv_count):
        total = total + exchange(shares[k], "kv", kv_count, k).astype(f32)
    packed = pack(0, page_cache, position, count, fold_key, packed)
    return packed, mass, attended, total.astype(bf16)


def solution(mesh):
    placed = (
        P("seq", None, "kv", None, None),
        P("seq", None),
        P("seq", None),
        P(),
        P(),
        P("seq", "kv", None),
        P("seq", None, "kv", None),
        P("kv", None),
    )
    return jax.shard_map(
        per_device,
        mesh=mesh,
        in_specs=placed,
        out_specs=(
            P("seq", None, "kv", None, None),
            P("seq", None),
            P("seq", "kv"),
            P("seq", "kv"),
        ),
        check_vma=False,
    )
```

```python
import functools

import jax
import jax.numpy as jnp
from jax import lax
from jax.experimental import pallas as pl
from jax.experimental.pallas import tpu as pltpu
from jax.sharding import PartitionSpec as P

negative_floor = -1e30
f32 = jnp.float32
bf16 = jnp.bfloat16
i32 = jnp.int32


def iota(shape, dim):
    return lax.broadcasted_iota(i32, shape, dim)


def dot(a, b, contract=(1, 0)):
    return lax.dot_general(
        a, b, (((contract[0],), (contract[1],)), ((), ())), preferred_element_type=f32
    )


def pieces(x):
    high = x.astype(bf16)
    rest = x - high.astype(f32)
    middle = rest.astype(bf16)
    low = (rest - middle.astype(f32)).astype(bf16)
    return high, middle, low


def ones_where(mask):
    return jnp.where(mask, 1.0, 0.0).astype(bf16)


def spread_rows(pages_dev, heads):
    rows = pages_dev * heads
    return ones_where(iota((rows, pages_dev), 0) // heads == iota((rows, pages_dev), 1))


def select_left(page, position, count_ref, slots):
    row = iota((slots, slots), 0).astype(f32)
    selector = ones_where(row == position[pl.ds(page, 1), :])
    return selector, row == count_ref[pl.ds(page, 1), :]


def share_rows(page, share):
    row = iota((16, share.shape[2]), 0)
    rows = jnp.zeros((16, share.shape[2]), f32)
    for n in range(3):
        rows = jnp.where(row == n, share[n, pl.ds(page, 1), :], rows)
    return rows.astype(bf16)


def rounded_fold(rows):
    return jnp.sum(rows, axis=0, keepdims=True).astype(bf16).astype(f32)


def side_by_side(ref, page):
    return jnp.concatenate([ref[page, g] for g in range(ref.shape[1])], axis=1)


def prepare_kernel(
    heads, req_dev, chunk, rank_ref, table_hbm, lengths_hbm, keep_hbm, weight_hbm, query_hbm,
    fresh_hbm, pages_hbm, keys, query_ref, fresh_ref, mass_ref, kept_ref, fold_mass_ref, position_ref, count_ref, share_ref,
    target_ref, slot_ref,
    table_ref, lengths_ref, keep_ref, weight_ref, small_sem, in_sem,
):
    pages_dev, slots = keep_ref.shape
    max_pages, reqs = table_ref.shape
    kv_local = keys.shape[1]
    chunks = pages_dev // chunk
    small = [
        pltpu.make_async_copy(a, b, small_sem.at[n])
        for n, (a, b) in enumerate(
            ((table_hbm, table_ref), (lengths_hbm, lengths_ref), (keep_hbm, keep_ref),
             (weight_hbm, weight_ref), (query_hbm, query_ref), (fresh_hbm, fresh_ref))
        )
    ]
    for copy in small:
        copy.start()
    loads = [
        pltpu.make_async_copy(
            pages_hbm.at[pl.ds(n * chunk, chunk), 0], keys.at[pl.ds(n * chunk, chunk)], in_sem.at[n]
        )
        for n in range(chunks)
    ]
    for copy in loads:
        copy.start()
    for copy in small:
        copy.wait()

    rank = rank_ref[0]
    page_id = iota((pages_dev, reqs), 0) + rank * pages_dev
    req_id = iota((pages_dev, reqs), 1)
    valid = jnp.zeros((pages_dev, reqs), i32)
    request = jnp.zeros((pages_dev, reqs), i32)
    for j in range(max_pages):
        match = table_ref[j : j + 1, :] == page_id
        left = jnp.clip(lengths_ref[...] - j * slots, 0, slots)
        valid = valid + jnp.where(match, left, 0)
        request = request + jnp.where(match, req_id, 0)
    valid = jnp.sum(valid, axis=1, keepdims=True)
    request = jnp.sum(request, axis=1, keepdims=True)
    slot_index = iota((pages_dev, slots), 1)
    in_page = slot_index < valid
    kept = jnp.logical_and(in_page, keep_ref[...] > 0)
    dropped = jnp.logical_and(in_page, keep_ref[...] == 0)
    kept_f = jnp.where(kept, 1.0, 0.0)
    before = ones_where(iota((slots, slots), 0) < iota((slots, slots), 1))
    position = dot(kept_f.astype(bf16), before)
    count = jnp.sum(kept_f, axis=1, keepdims=True)
    dropped_weight = jnp.where(dropped, weight_ref[...], 0.0)
    weight_sum = jnp.sum(dropped_weight, axis=1, keepdims=True)
    slot_f = slot_index.astype(f32)
    mass_ref[...] = jnp.where(
        slot_f < count, 1.0, jnp.where(slot_f == count, weight_sum, 0.0)
    ).astype(bf16)
    kept_ref[...] = kept_f
    fold_mass_ref[...] = jnp.broadcast_to(weight_sum.astype(bf16).astype(f32), (pages_dev, slots))
    position_ref[...] = jnp.where(kept, position, -1.0)
    count_ref[...] = jnp.broadcast_to(count, (pages_dev, slots))
    share = pieces(dropped_weight / jnp.maximum(weight_sum, 1.0))
    for n in range(3):
        share_ref[n] = share[n].astype(f32)

    owner = request // req_dev
    chip, core = owner // 2, owner % 2
    chips = reqs // req_dev // 2
    from_chip = lax.rem(rank // 2 - chip + chips, chips)
    from_core = jnp.where(core == rank % 2, 0, 1)
    at_hand = (from_core * (reqs // req_dev // 2) + from_chip) * req_dev + request % req_dev
    at_hand = jnp.broadcast_to(at_hand, (pages_dev, slots)).astype(f32)
    spread = spread_rows(pages_dev, heads)
    rows = pages_dev * heads
    target_ref[...] = dot(spread, at_hand.astype(bf16)).astype(i32) * heads + iota((rows, slots), 0) % heads
    owner_col = jnp.broadcast_to(owner, (pages_dev, pages_dev))
    page_row, page_col = iota((pages_dev, pages_dev), 0), iota((pages_dev, pages_dev), 1)
    owner_row = jnp.sum(jnp.where(page_row == page_col, owner_col, 0), axis=0, keepdims=True)
    earlier = jnp.logical_and(owner_col == owner_row, page_row < page_col)
    order = jnp.sum(jnp.where(earlier, 1, 0), axis=0, keepdims=True)
    slot = owner_row * (pages_dev // (reqs // req_dev)) + order
    slot = jnp.broadcast_to(slot, (8, pages_dev)).astype(f32).astype(bf16)
    slot_ref[...] = dot(slot, spread, (1, 1))

    for copy in loads:
        copy.wait()


def prepare(rank, page_table, lengths, keep_list, fold_weight, queries, fresh_entries, page_cache, heads, req_dev, chunk=16):
    pages_dev, _, kv_local, slots, head_size = page_cache.shape
    reqs, max_pages = page_table.shape
    rows = pages_dev * heads
    chunks = pages_dev // chunk
    hbm = pl.BlockSpec(memory_space=pltpu.HBM)
    vmem = pl.BlockSpec(memory_space=pltpu.VMEM)
    small = (pages_dev, slots)
    return pl.pallas_call(
        functools.partial(prepare_kernel, heads, req_dev, chunk),
        in_specs=[pl.BlockSpec(memory_space=pltpu.SMEM)] + [hbm] * 7,
        out_specs=[vmem] * 11,
        out_shape=[
            pltpu.VMEM((pages_dev, kv_local, slots, head_size), bf16),
            pltpu.VMEM(queries.shape, bf16),
            pltpu.VMEM(fresh_entries.shape, bf16),
            jax.ShapeDtypeStruct(small, bf16),
            jax.ShapeDtypeStruct(small, f32),
            jax.ShapeDtypeStruct(small, f32),
            jax.ShapeDtypeStruct(small, f32),
            jax.ShapeDtypeStruct(small, f32),
            jax.ShapeDtypeStruct((3,) + small, f32),
            jax.ShapeDtypeStruct((rows, slots), i32),
            jax.ShapeDtypeStruct((8, rows), f32),
        ],
        scratch_shapes=[
            pltpu.VMEM((max_pages, reqs), i32),
            pltpu.VMEM((1, reqs), i32),
            pltpu.VMEM(small, i32),
            pltpu.VMEM(small, f32),
            pltpu.SemaphoreType.DMA((6,)),
            pltpu.SemaphoreType.DMA((chunks,)),
        ],
        compiler_params=pltpu.CompilerParams(vmem_limit_bytes=24 << 20),
        name="prepare",
    )(
        rank, *(
            pltpu.with_memory_space_constraint(x, pltpu.HBM)
            for x in (
                page_table.T, lengths.reshape(1, -1), keep_list, fold_weight, queries, fresh_entries,
                page_cache,
            )
        )
    )


def fold_kernel(keys, share_ref, folded_ref, _):
    pages_dev, kv_local = keys.shape[:2]
    for page in range(pages_dev):
        result = dot(share_rows(page, share_ref), side_by_side(keys, page))
        folded = rounded_fold(result[:8])
        for g in range(kv_local):
            folded_ref[g, page : page + 1, :] = folded[:, g * 128 : (g + 1) * 128]


def fold_keys(keys, share):
    pages_dev, kv_local, _, head_size = keys.shape
    vmem = pl.BlockSpec(memory_space=pltpu.VMEM)
    return pl.pallas_call(
        fold_kernel,
        in_specs=[vmem] * 2,
        out_specs=[vmem] * 2,
        out_shape=[
            jax.ShapeDtypeStruct((kv_local, pages_dev, head_size), f32),
            pltpu.VMEM(keys.shape, bf16),
        ],
        input_output_aliases={0: 1},
        compiler_params=pltpu.CompilerParams(vmem_limit_bytes=24 << 20),
        name="fold_keys",
    )(keys, share)


def pack_kernel(spans, chunk, pages_hbm, position_ref, count_ref, *rest):
    folded_refs = rest[:2]
    packed_hbm, raw, staged, in_sem, out_sem = rest[-5:]
    slots = position_ref.shape[1]
    kv_local = raw.shape[1]
    parts = [(half, n) for half, first, end in spans for n in range(first, end, chunk)]
    loads, stores = [], []
    for i, (half, n) in enumerate(parts):
        there, here = pl.ds(n, chunk), pl.ds(i * chunk, chunk)
        loads.append(
            pltpu.make_async_copy(pages_hbm.at[there, half], raw.at[here], in_sem.at[i])
        )
        stores.append(
            pltpu.make_async_copy(staged.at[here], packed_hbm.at[there, half], out_sem.at[i])
        )
    for copy in loads:
        copy.start()
    for i, (half, n) in enumerate(parts):
        loads[i].wait()
        for j in range(chunk):
            page, at = n + j, i * chunk + j
            selector, at_fold = select_left(page, position_ref, count_ref, slots)
            result = dot(selector, side_by_side(raw, at))
            for g in range(kv_local):
                staged[at, g] = jnp.where(
                    at_fold, folded_refs[half][g, pl.ds(page, 1), :],
                    result[:, g * 128 : (g + 1) * 128],
                ).astype(bf16)
        stores[i].start()
    for copy in stores:
        copy.wait()


def pack(name, spans, page_cache, position, count, fold_key, fold_value, packed=None, chunk=8):
    _, _, kv_local, slots, head_size = page_cache.shape
    hbm = pl.BlockSpec(memory_space=pltpu.HBM)
    vmem = pl.BlockSpec(memory_space=pltpu.VMEM)
    size = sum(end - first for _, first, end in spans)
    buffer = pltpu.VMEM((size, kv_local, slots, head_size), bf16)
    chunks = pltpu.SemaphoreType.DMA((size // chunk,))
    in_hbm = lambda x: pltpu.with_memory_space_constraint(x, pltpu.HBM)
    there = [] if packed is None else [in_hbm(packed)]
    return pl.pallas_call(
        functools.partial(pack_kernel, spans, chunk),
        in_specs=[hbm] + [vmem] * 4 + [hbm] * len(there),
        out_specs=hbm,
        out_shape=jax.ShapeDtypeStruct(page_cache.shape, bf16),
        input_output_aliases={5: 0} if there else {},
        scratch_shapes=[buffer, buffer, chunks, chunks],
        compiler_params=pltpu.CompilerParams(vmem_limit_bytes=24 << 20),
        name=name,
    )(in_hbm(page_cache), position, count, fold_key, fold_value, *there)


def attend_kernel(
    heads, req_dev, score_scale, chunk, chips, keys, kept_ref, fold_mass_ref, share_ref,
    fold_key_ref, target_ref, slot_ref, pages_hbm, *rest,
):
    pages_dev, slots = kept_ref.shape
    query_refs = rest[: 2 * chips]
    out_ref, fold_value_ref, values, scores, parts, value_sem = rest[2 * chips :]
    kv_local = keys.shape[1]
    loads = [
        pltpu.make_async_copy(
            pages_hbm.at[pl.ds(n * chunk, chunk), 1], values.at[pl.ds(n * chunk, chunk)],
            value_sem.at[n],
        )
        for n in range(pages_dev // chunk)
    ]
    for copy in loads:
        copy.start()
    groups = heads // kv_local
    rows = pages_dev * heads
    spread = spread_rows(pages_dev, heads)

    query = jnp.zeros((rows, 128), f32)
    per_slab = slots // query_refs[0].shape[0]
    for n in range(0, 2 * chips, per_slab):
        slab = jnp.concatenate([ref[...] for ref in query_refs[n : n + per_slab]], axis=0)
        first = n * query_refs[0].shape[0]
        pick = ones_where(target_ref[...] == iota((rows, slots), 1) + first)
        query = query + dot(pick, slab)
    query_b = query.astype(bf16)

    tile = 16
    tile_pages = tile // heads
    row = iota((tile, 128), 0)
    row_page = row // heads
    row_group = (row % heads) // groups

    def choose(results):
        chosen = results[0][:tile, :128]
        for i in range(tile_pages):
            for g in range(kv_local):
                if i + g > 0:
                    here = jnp.logical_and(row_page == i, row_group == g)
                    chosen = jnp.where(here, results[i][:tile, g * 128 : (g + 1) * 128], chosen)
        return chosen

    for first in range(0, pages_dev, tile_pages):
        at = first * heads
        left = query_b[at : at + tile]
        results = [
            dot(left, keys[first + i].reshape(kv_local * slots, 128), (1, 1))
            for i in range(tile_pages)
        ]
        scores[at : at + tile, :] = choose(results)

    group_of = (iota((rows, pages_dev), 0) % heads) // groups
    spread_g = [
        jnp.where(group_of == g, spread.astype(f32), 0.0).astype(bf16) for g in range(kv_local)
    ]

    def spread_fold(ref):
        return sum(dot(spread_g[g], ref[g].astype(bf16)) for g in range(kv_local))

    kept = dot(spread, kept_ref[...].astype(bf16)) > 0.5
    fold_mass = dot(spread, fold_mass_ref[...].astype(bf16))[:, :1]
    fold_score = jnp.sum(query * spread_fold(fold_key_ref), axis=1, keepdims=True) * score_scale
    fold_live = fold_mass > 0
    score = jnp.where(kept, scores[...] * score_scale, negative_floor)
    top = jnp.maximum(
        jnp.max(score, axis=1, keepdims=True), jnp.where(fold_live, fold_score, negative_floor)
    )
    weight = jnp.where(kept, jnp.exp(score - top), 0.0)
    fold_weight = jnp.where(fold_live, fold_mass * jnp.exp(fold_score - top), 0.0)
    total = jnp.sum(weight, axis=1, keepdims=True) + fold_weight
    weight_b = weight.astype(bf16)

    for first in range(0, pages_dev, tile_pages):
        if first % chunk == 0:
            loads[first // chunk].wait()
        at = first * heads
        results = []
        for i in range(tile_pages):
            left = jnp.concatenate(
                [weight_b[at : at + tile], share_rows(first + i, share_ref)], axis=0
            )
            result = dot(left, side_by_side(values, first + i))
            results.append(result)
            folded = rounded_fold(result[tile : tile + 8])
            for g in range(kv_local):
                fold_value_ref[g, first + i : first + i + 1, :] = folded[:, g * 128 : (g + 1) * 128]
        parts[at : at + tile, :] = choose(results)

    part = parts[...] + fold_weight.astype(bf16).astype(f32) * spread_fold(fold_value_ref)
    lane = iota((rows, 128), 1)
    local = (target_ref[...] // heads % req_dev).astype(f32)
    stats = jnp.where(lane == 6, local, 0.0)
    for n, piece in enumerate(pieces(top) + pieces(total)):
        stats = jnp.where(lane == n, piece.astype(f32), stats)
    send = jnp.concatenate([part.astype(bf16), stats.astype(bf16)], axis=1)
    place = slot_ref[:1] * heads + (iota((1, rows), 1) % heads).astype(f32)
    move = ones_where(iota((rows, rows), 0).astype(f32) == place)
    out_ref[...] = dot(move, send).astype(bf16)


def attend(
    near, far, keys, kept, fold_mass, share, fold_key, target, slot, page_cache, score_scale, heads,
    req_dev, chips, chunk=16
):
    pages_dev, _, kv_local, slots, head_size = page_cache.shape
    rows = pages_dev * heads
    vmem = pl.BlockSpec(memory_space=pltpu.VMEM)
    return pl.pallas_call(
        functools.partial(attend_kernel, heads, req_dev, score_scale, chunk, chips),
        in_specs=[vmem] * 7 + [pl.BlockSpec(memory_space=pltpu.HBM)] + [vmem] * (2 * chips),
        out_specs=[vmem] * 2,
        out_shape=[
            jax.ShapeDtypeStruct((rows, 2 * head_size), bf16),
            jax.ShapeDtypeStruct((kv_local, pages_dev, head_size), f32),
        ],
        scratch_shapes=[
            pltpu.VMEM((pages_dev, kv_local, slots, head_size), bf16),
            pltpu.VMEM((rows, slots), f32),
            pltpu.VMEM((rows, head_size), f32),
            pltpu.SemaphoreType.DMA((pages_dev // chunk,)),
        ],
        compiler_params=pltpu.CompilerParams(vmem_limit_bytes=24 << 20),
        name="attend",
    )(
        keys, kept, fold_mass, share, fold_key, target, slot,
        pltpu.with_memory_space_constraint(page_cache, pltpu.HBM), *near, *far,
    )


def combine_kernel(
    heads, kv_local, req_dev, score_scale, kv_count, rank_ref, query_ref, fresh_ref,
    weight_ref, *rest
):
    got_ref, attended_ref, *out_refs = rest
    got = got_ref[...]
    rows = got.shape[0]
    cols = heads * req_dev
    width = weight_ref.shape[1] // kv_count
    stats = got[:, 128:].astype(f32)
    top = stats[:, 0:1] + stats[:, 1:2] + stats[:, 2:3]
    request = stats[:, 6:7]
    row_head = (iota((rows, cols), 0) % heads).astype(f32)
    col = iota((rows, cols), 1)
    match = jnp.logical_and(
        request == (col % req_dev).astype(f32), row_head == (col // req_dev).astype(f32)
    )
    head, request = iota((cols, 1), 0) // req_dev, iota((cols, 1), 0) % req_dev

    def rows_of(ref, index):
        return dot(ones_where(iota((cols, ref.shape[0]), 1) == index), ref[...])

    fresh_row = request * (2 * kv_local) + head // (heads // kv_local)
    own = jnp.sum(
        rows_of(query_ref, request * heads + head) * rows_of(fresh_ref, fresh_row),
        axis=1, keepdims=True,
    ) * score_scale
    diagonal = iota((cols, cols), 0) == iota((cols, cols), 1)
    own_row = jnp.sum(jnp.where(diagonal, own, 0.0), axis=0, keepdims=True)
    best = jnp.maximum(
        jnp.max(jnp.where(match, top, negative_floor), axis=0, keepdims=True), own_row
    )
    best_col = jnp.sum(jnp.where(diagonal, best, 0.0), axis=1, keepdims=True)
    factor = jnp.where(match, jnp.exp(top - best), 0.0)
    high, middle, low = pieces(factor)
    sums = dot(high, got, (0, 0)) + dot(middle, got, (0, 0)) + dot(low, got, (0, 0))
    own_factor = jnp.exp(own - best_col)
    denominator = sums[:, 131:132] + sums[:, 132:133] + sums[:, 133:134] + own_factor
    numerator = sums[:, :128] + own_factor * rows_of(fresh_ref, fresh_row + kv_local)
    attended = numerator / denominator
    attended = jnp.concatenate(
        [attended[h * req_dev : (h + 1) * req_dev] for h in range(heads)], axis=1
    ).astype(bf16)
    attended_ref[...] = attended
    rank = rank_ref[0]
    for k in range(kv_count):
        other = jnp.bitwise_xor(rank, k)
        at = pl.multiple_of(other * width, width)
        out_refs[k][...] = dot(attended, weight_ref[:, pl.ds(at, width)]).astype(bf16)


def combine(rank, got, query, fresh, out_weight, score_scale, heads, kv_local, kv_count):
    req_dev = query.shape[0] // heads
    vmem = pl.BlockSpec(memory_space=pltpu.VMEM)
    smem = pl.BlockSpec(memory_space=pltpu.SMEM)
    width = out_weight.shape[1] // kv_count
    return pl.pallas_call(
        functools.partial(combine_kernel, heads, kv_local, req_dev, score_scale, kv_count),
        in_specs=[smem] + [vmem] * 4,
        out_specs=[vmem] * (1 + kv_count),
        out_shape=[jax.ShapeDtypeStruct((req_dev, out_weight.shape[0]), bf16)]
        + [jax.ShapeDtypeStruct((req_dev, width), bf16)] * kv_count,
        compiler_params=pltpu.CompilerParams(vmem_limit_bytes=24 << 20),
        cost_estimate=pl.CostEstimate(
            flops=2 * req_dev * out_weight.size, bytes_accessed=2 * out_weight.size, transcendentals=0
        ),
        name="combine",
    )(rank, query, fresh, out_weight, got)


def exchange(x, axis, count, mask):
    return lax.ppermute(x, axis, [(i, i ^ mask) for i in range(count)])


def shift(x, axis, count, step):
    return lax.ppermute(x, axis, [(i, (i + step) % count) for i in range(count)])


def per_device(
    page_cache, keep_list, fold_weight, page_table, lengths, queries, fresh_entries, out_weight
):
    seq_count = lax.axis_size("seq")
    kv_count = lax.axis_size("kv")
    assert seq_count & (seq_count - 1) == 0 and kv_count & (kv_count - 1) == 0
    seq_rank = lax.axis_index("seq").astype(i32).reshape(1)
    kv_rank = lax.axis_index("kv").astype(i32).reshape(1)
    _, _, kv_local, slots, head_size = page_cache.shape
    req_dev, heads, _ = queries.shape
    score_scale = head_size ** (-0.5)

    others = {k: shift(queries, "seq", seq_count, 2 * k) for k in [2] + [k for k in range(seq_count // 2 - 1, 0, -1) if k != 2]}
    others = [others[k] for k in range(1, seq_count // 2)]
    keys, own, fresh, mass, kept, fold_mass, position, count, share, target, slot = prepare(
        seq_rank, page_table, lengths, keep_list, fold_weight, queries, fresh_entries, page_cache,
        heads, req_dev,
    )
    flat = lambda x: x.reshape(-1, head_size)
    near = [flat(x) for x in [own] + others]
    far = [exchange(x, "seq", seq_count, 1) for x in near]
    fold_key, keys = fold_keys(keys, share)
    fold_key, *far = lax.optimization_barrier((fold_key, *far))
    send, fold_value = attend(
        near, far, keys, kept, fold_mass, share, fold_key, target, slot, page_cache, score_scale,
        heads, req_dev, seq_count // 2,
    )
    got = lax.all_to_all(
        send.reshape(seq_count, -1, send.shape[1]), "seq", split_axis=0, concat_axis=0, tiled=True
    ).reshape(send.shape)
    pages_dev = page_cache.shape[0]
    fold_key, fold_value = lax.optimization_barrier((fold_key, fold_value))
    middle = pages_dev // 2
    packed = pack(
        "pack_first", [(0, 0, pages_dev), (1, 0, middle)], page_cache, position, count, fold_key,
        fold_value,
    )
    got, packed = lax.optimization_barrier((got, packed))
    attended, *shares = combine(
        kv_rank, got, flat(own), flat(fresh), out_weight, score_scale, heads, kv_local, kv_count,
    )
    packed, *shares = lax.optimization_barrier((packed, *shares))
    packed = pack(
        "pack_rest", [(1, middle, pages_dev)], page_cache, position, count, fold_key, fold_value, packed
    )
    total = shares[0].astype(f32)
    for k in range(kv_count - 1, 0, -1):
        total = total + exchange(shares[k], "kv", kv_count, k).astype(f32)
    return packed, mass, attended, total.astype(bf16)


def solution(mesh):
    placed = (
        P("seq", None, "kv", None, None),
        P("seq", None),
        P("seq", None),
        P(),
        P(),
        P("seq", "kv", None),
        P("seq", None, "kv", None),
        P("kv", None),
    )
    return jax.shard_map(
        per_device,
        mesh=mesh,
        in_specs=placed,
        out_specs=(
            P("seq", None, "kv", None, None),
            P("seq", None),
            P("seq", "kv"),
            P("seq", "kv"),
        ),
        check_vma=False,
    )
```

```python
import functools

import jax
import jax.numpy as jnp
from jax import lax
from jax.experimental import pallas as pl
from jax.experimental.pallas import tpu as pltpu
from jax.sharding import PartitionSpec as P

negative_floor = -1e30
f32 = jnp.float32
bf16 = jnp.bfloat16
i32 = jnp.int32


def iota(shape, dim):
    return lax.broadcasted_iota(i32, shape, dim)


def dot(a, b, contract=(1, 0)):
    return lax.dot_general(
        a, b, (((contract[0],), (contract[1],)), ((), ())), preferred_element_type=f32
    )


def pieces(x):
    high = x.astype(bf16)
    rest = x - high.astype(f32)
    middle = rest.astype(bf16)
    low = (rest - middle.astype(f32)).astype(bf16)
    return high, middle, low


def ones_where(mask):
    return jnp.where(mask, 1.0, 0.0).astype(bf16)


def spread_rows(pages_dev, heads):
    rows = pages_dev * heads
    return ones_where(iota((rows, pages_dev), 0) // heads == iota((rows, pages_dev), 1))


def select_left(page, position, count_ref, slots):
    row = iota((slots, slots), 0).astype(f32)
    selector = ones_where(row == position[pl.ds(page, 1), :])
    return selector, row == count_ref[pl.ds(page, 1), :]


def share_rows(page, share):
    row = iota((16, share.shape[2]), 0)
    rows = jnp.zeros((16, share.shape[2]), f32)
    for n in range(3):
        rows = jnp.where(row == n, share[n, pl.ds(page, 1), :], rows)
    return rows.astype(bf16)


def rounded_fold(rows):
    return jnp.sum(rows, axis=0, keepdims=True).astype(bf16).astype(f32)


def side_by_side(ref, page):
    return jnp.concatenate([ref[page, g] for g in range(ref.shape[1])], axis=1)


def prepare_kernel(
    heads, req_dev, chunk, rank_ref, table_hbm, lengths_hbm, keep_hbm, weight_hbm, query_hbm,
    fresh_hbm, pages_hbm, keys, values, query_ref, fresh_ref, mass_ref, kept_ref, fold_mass_ref, position_ref, count_ref, share_ref,
    target_ref, slot_ref,
    table_ref, lengths_ref, keep_ref, weight_ref, small_sem, in_sem,
):
    pages_dev, slots = keep_ref.shape
    max_pages, reqs = table_ref.shape
    kv_local = keys.shape[1]
    chunks = pages_dev // chunk
    small = [
        pltpu.make_async_copy(a, b, small_sem.at[n])
        for n, (a, b) in enumerate(
            ((table_hbm, table_ref), (lengths_hbm, lengths_ref), (keep_hbm, keep_ref),
             (weight_hbm, weight_ref), (query_hbm, query_ref), (fresh_hbm, fresh_ref))
        )
    ]
    for copy in small:
        copy.start()
    loads = [
        pltpu.make_async_copy(
            pages_hbm.at[pl.ds(n * chunk, chunk), half], held.at[pl.ds(n * chunk, chunk)],
            in_sem.at[half, n],
        )
        for half, held in enumerate((keys, values))
        for n in range(chunks)
    ]
    for copy in loads:
        copy.start()
    for copy in small:
        copy.wait()

    rank = rank_ref[0]
    page_id = iota((pages_dev, reqs), 0) + rank * pages_dev
    req_id = iota((pages_dev, reqs), 1)
    valid = jnp.zeros((pages_dev, reqs), i32)
    request = jnp.zeros((pages_dev, reqs), i32)
    for j in range(max_pages):
        match = table_ref[j : j + 1, :] == page_id
        left = jnp.clip(lengths_ref[...] - j * slots, 0, slots)
        valid = valid + jnp.where(match, left, 0)
        request = request + jnp.where(match, req_id, 0)
    valid = jnp.sum(valid, axis=1, keepdims=True)
    request = jnp.sum(request, axis=1, keepdims=True)
    slot_index = iota((pages_dev, slots), 1)
    in_page = slot_index < valid
    kept = jnp.logical_and(in_page, keep_ref[...] > 0)
    dropped = jnp.logical_and(in_page, keep_ref[...] == 0)
    kept_f = jnp.where(kept, 1.0, 0.0)
    before = ones_where(iota((slots, slots), 0) < iota((slots, slots), 1))
    position = dot(kept_f.astype(bf16), before)
    count = jnp.sum(kept_f, axis=1, keepdims=True)
    dropped_weight = jnp.where(dropped, weight_ref[...], 0.0)
    weight_sum = jnp.sum(dropped_weight, axis=1, keepdims=True)
    slot_f = slot_index.astype(f32)
    mass_ref[...] = jnp.where(
        slot_f < count, 1.0, jnp.where(slot_f == count, weight_sum, 0.0)
    ).astype(bf16)
    kept_ref[...] = kept_f
    fold_mass_ref[...] = jnp.broadcast_to(weight_sum.astype(bf16).astype(f32), (pages_dev, slots))
    position_ref[...] = jnp.where(kept, position, -1.0)
    count_ref[...] = jnp.broadcast_to(count, (pages_dev, slots))
    share = pieces(dropped_weight / jnp.maximum(weight_sum, 1.0))
    for n in range(3):
        share_ref[n] = share[n].astype(f32)

    owner = request // req_dev
    chip, core = owner // 2, owner % 2
    chips = reqs // req_dev // 2
    from_chip = lax.rem(rank // 2 - chip + chips, chips)
    from_core = jnp.where(core == rank % 2, 0, 1)
    at_hand = (from_core * (reqs // req_dev // 2) + from_chip) * req_dev + request % req_dev
    at_hand = jnp.broadcast_to(at_hand, (pages_dev, slots)).astype(f32)
    spread = spread_rows(pages_dev, heads)
    rows = pages_dev * heads
    target_ref[...] = dot(spread, at_hand.astype(bf16)).astype(i32) * heads + iota((rows, slots), 0) % heads
    owner_col = jnp.broadcast_to(owner, (pages_dev, pages_dev))
    page_row, page_col = iota((pages_dev, pages_dev), 0), iota((pages_dev, pages_dev), 1)
    owner_row = jnp.sum(jnp.where(page_row == page_col, owner_col, 0), axis=0, keepdims=True)
    earlier = jnp.logical_and(owner_col == owner_row, page_row < page_col)
    order = jnp.sum(jnp.where(earlier, 1, 0), axis=0, keepdims=True)
    slot = owner_row * (pages_dev // (reqs // req_dev)) + order
    slot = jnp.broadcast_to(slot, (8, pages_dev)).astype(f32).astype(bf16)
    slot_ref[...] = dot(slot, spread, (1, 1))

    for copy in loads:
        copy.wait()


def prepare(rank, page_table, lengths, keep_list, fold_weight, queries, fresh_entries, page_cache, heads, req_dev, chunk=16):
    pages_dev, _, kv_local, slots, head_size = page_cache.shape
    reqs, max_pages = page_table.shape
    rows = pages_dev * heads
    chunks = pages_dev // chunk
    hbm = pl.BlockSpec(memory_space=pltpu.HBM)
    vmem = pl.BlockSpec(memory_space=pltpu.VMEM)
    small = (pages_dev, slots)
    return pl.pallas_call(
        functools.partial(prepare_kernel, heads, req_dev, chunk),
        in_specs=[pl.BlockSpec(memory_space=pltpu.SMEM)] + [hbm] * 7,
        out_specs=[vmem] * 12,
        out_shape=[
            pltpu.VMEM((pages_dev, kv_local, slots, head_size), bf16),
            pltpu.VMEM((pages_dev, kv_local, slots, head_size), bf16),
            pltpu.VMEM(queries.shape, bf16),
            pltpu.VMEM(fresh_entries.shape, bf16),
            jax.ShapeDtypeStruct(small, bf16),
            jax.ShapeDtypeStruct(small, f32),
            jax.ShapeDtypeStruct(small, f32),
            jax.ShapeDtypeStruct(small, f32),
            jax.ShapeDtypeStruct(small, f32),
            jax.ShapeDtypeStruct((3,) + small, f32),
            jax.ShapeDtypeStruct((rows, slots), i32),
            jax.ShapeDtypeStruct((8, rows), f32),
        ],
        scratch_shapes=[
            pltpu.VMEM((max_pages, reqs), i32),
            pltpu.VMEM((1, reqs), i32),
            pltpu.VMEM(small, i32),
            pltpu.VMEM(small, f32),
            pltpu.SemaphoreType.DMA((6,)),
            pltpu.SemaphoreType.DMA((2, chunks)),
        ],
        compiler_params=pltpu.CompilerParams(vmem_limit_bytes=24 << 20),
        name="prepare",
    )(
        rank, *(
            pltpu.with_memory_space_constraint(x, pltpu.HBM)
            for x in (
                page_table.T, lengths.reshape(1, -1), keep_list, fold_weight, queries, fresh_entries,
                page_cache,
            )
        )
    )


def fold_kernel(keys, share_ref, folded_ref, _):
    pages_dev, kv_local = keys.shape[:2]
    for page in range(pages_dev):
        result = dot(share_rows(page, share_ref), side_by_side(keys, page))
        folded = rounded_fold(result[:8])
        for g in range(kv_local):
            folded_ref[g, page : page + 1, :] = folded[:, g * 128 : (g + 1) * 128]


def fold_keys(keys, share):
    pages_dev, kv_local, _, head_size = keys.shape
    vmem = pl.BlockSpec(memory_space=pltpu.VMEM)
    return pl.pallas_call(
        fold_kernel,
        in_specs=[vmem] * 2,
        out_specs=[vmem] * 2,
        out_shape=[
            jax.ShapeDtypeStruct((kv_local, pages_dev, head_size), f32),
            pltpu.VMEM(keys.shape, bf16),
        ],
        input_output_aliases={0: 1},
        compiler_params=pltpu.CompilerParams(vmem_limit_bytes=24 << 20),
        name="fold_keys",
    )(keys, share)


def pack_kernel(spans, chunk, pages_hbm, position_ref, count_ref, *rest):
    folded_refs = rest[:2]
    packed_hbm, raw, staged, in_sem, out_sem = rest[-5:]
    slots = position_ref.shape[1]
    kv_local = raw.shape[1]
    parts = [(half, n) for half, first, end in spans for n in range(first, end, chunk)]
    loads, stores = [], []
    for i, (half, n) in enumerate(parts):
        there, here = pl.ds(n, chunk), pl.ds(i * chunk, chunk)
        loads.append(
            pltpu.make_async_copy(pages_hbm.at[there, half], raw.at[here], in_sem.at[i])
        )
        stores.append(
            pltpu.make_async_copy(staged.at[here], packed_hbm.at[there, half], out_sem.at[i])
        )
    for copy in loads:
        copy.start()
    for i, (half, n) in enumerate(parts):
        loads[i].wait()
        for j in range(chunk):
            page, at = n + j, i * chunk + j
            selector, at_fold = select_left(page, position_ref, count_ref, slots)
            result = dot(selector, side_by_side(raw, at))
            for g in range(kv_local):
                staged[at, g] = jnp.where(
                    at_fold, folded_refs[half][g, pl.ds(page, 1), :],
                    result[:, g * 128 : (g + 1) * 128],
                ).astype(bf16)
        stores[i].start()
    for copy in stores:
        copy.wait()


def pack(name, spans, page_cache, position, count, fold_key, fold_value, packed=None, chunk=8):
    _, _, kv_local, slots, head_size = page_cache.shape
    hbm = pl.BlockSpec(memory_space=pltpu.HBM)
    vmem = pl.BlockSpec(memory_space=pltpu.VMEM)
    size = sum(end - first for _, first, end in spans)
    buffer = pltpu.VMEM((size, kv_local, slots, head_size), bf16)
    chunks = pltpu.SemaphoreType.DMA((size // chunk,))
    in_hbm = lambda x: pltpu.with_memory_space_constraint(x, pltpu.HBM)
    there = [] if packed is None else [in_hbm(packed)]
    return pl.pallas_call(
        functools.partial(pack_kernel, spans, chunk),
        in_specs=[hbm] + [vmem] * 4 + [hbm] * len(there),
        out_specs=hbm,
        out_shape=jax.ShapeDtypeStruct(page_cache.shape, bf16),
        input_output_aliases={5: 0} if there else {},
        scratch_shapes=[buffer, buffer, chunks, chunks],
        compiler_params=pltpu.CompilerParams(vmem_limit_bytes=24 << 20),
        name=name,
    )(in_hbm(page_cache), position, count, fold_key, fold_value, *there)


def message(rows, peers):
    each = rows // peers
    return (peers * (each + each // 4), 128) if each % 32 == 0 else (rows, 256)


def attend_kernel(
    heads, req_dev, score_scale, peers, keys, kept_ref, fold_mass_ref, share_ref,
    fold_key_ref, target_ref, slot_ref, values, *rest,
):
    pages_dev, slots = kept_ref.shape
    query_refs = rest[:2]
    out_ref, fold_value_ref, scores, parts = rest[2:]
    kv_local = keys.shape[1]
    groups = heads // kv_local
    rows = pages_dev * heads
    spread = spread_rows(pages_dev, heads)

    query = jnp.zeros((rows, 128), f32)
    held = jnp.concatenate([ref[...] for ref in query_refs], axis=0)
    for first in range(0, held.shape[0], slots):
        pick = ones_where(target_ref[...] == iota((rows, slots), 1) + first)
        query = query + dot(pick, held[first : first + slots])
    query_b = query.astype(bf16)

    tile = 16
    tile_pages = tile // heads
    row = iota((tile, 128), 0)
    row_page = row // heads
    row_group = (row % heads) // groups

    def choose(results):
        chosen = results[0][:tile, :128]
        for i in range(tile_pages):
            for g in range(kv_local):
                if i + g > 0:
                    here = jnp.logical_and(row_page == i, row_group == g)
                    chosen = jnp.where(here, results[i][:tile, g * 128 : (g + 1) * 128], chosen)
        return chosen

    for first in range(0, pages_dev, tile_pages):
        at = first * heads
        left = query_b[at : at + tile]
        results = [
            dot(left, keys[first + i].reshape(kv_local * slots, 128), (1, 1))
            for i in range(tile_pages)
        ]
        scores[at : at + tile, :] = choose(results)

    group_of = (iota((rows, pages_dev), 0) % heads) // groups
    spread_g = [
        jnp.where(group_of == g, spread.astype(f32), 0.0).astype(bf16) for g in range(kv_local)
    ]

    def spread_fold(ref):
        return sum(dot(spread_g[g], ref[g].astype(bf16)) for g in range(kv_local))

    kept = dot(spread, kept_ref[...].astype(bf16)) > 0.5
    fold_mass = dot(spread, fold_mass_ref[...].astype(bf16))[:, :1]
    fold_score = jnp.sum(query * spread_fold(fold_key_ref), axis=1, keepdims=True) * score_scale
    fold_live = fold_mass > 0
    score = jnp.where(kept, scores[...] * score_scale, negative_floor)
    top = jnp.maximum(
        jnp.max(score, axis=1, keepdims=True), jnp.where(fold_live, fold_score, negative_floor)
    )
    weight = jnp.where(kept, jnp.exp(score - top), 0.0)
    fold_weight = jnp.where(fold_live, fold_mass * jnp.exp(fold_score - top), 0.0)
    total = jnp.sum(weight, axis=1, keepdims=True) + fold_weight
    weight_b = weight.astype(bf16)

    for first in range(0, pages_dev, tile_pages):
        at = first * heads
        results = []
        for i in range(tile_pages):
            left = jnp.concatenate(
                [weight_b[at : at + tile], share_rows(first + i, share_ref)], axis=0
            )
            result = dot(left, side_by_side(values, first + i))
            results.append(result)
            folded = rounded_fold(result[tile : tile + 8])
            for g in range(kv_local):
                fold_value_ref[g, first + i : first + i + 1, :] = folded[:, g * 128 : (g + 1) * 128]
        parts[at : at + tile, :] = choose(results)

    part = parts[...] + fold_weight.astype(bf16).astype(f32) * spread_fold(fold_value_ref)
    lane = iota((rows, 128), 1)
    local = (target_ref[...] // heads % req_dev).astype(f32)
    stats = jnp.where(lane == 6, local, 0.0)
    for n, piece in enumerate(pieces(top) + pieces(total)):
        stats = jnp.where(lane == n, piece.astype(f32), stats)
    send = jnp.concatenate([part.astype(bf16), stats.astype(bf16)], axis=1)
    place = slot_ref[:1] * heads + (iota((1, rows), 1) % heads).astype(f32)
    move = ones_where(iota((rows, rows), 0).astype(f32) == place)
    placed = dot(move, send)
    each = rows // peers
    if out_ref.shape[1] == 256:
        out_ref[...] = placed.astype(bf16)
    else:
        quarter = each // 4
        message_rows = []
        for n in range(peers):
            mine = placed[n * each : (n + 1) * each]
            message_rows.append(mine[:, :128])
            message_rows.append(
                mine[:quarter, 128:]
                + sum(
                    jnp.roll(mine[k * quarter : (k + 1) * quarter, 128:], 32 * k, axis=1)
                    for k in range(1, 4)
                )
            )
        out_ref[...] = jnp.concatenate(message_rows, axis=0).astype(bf16)


def attend(
    near, far, keys, kept, fold_mass, share, fold_key, target, slot, values, score_scale, heads,
    req_dev, peers
):
    pages_dev, kv_local, slots, head_size = values.shape
    rows = pages_dev * heads
    vmem = pl.BlockSpec(memory_space=pltpu.VMEM)
    return pl.pallas_call(
        functools.partial(attend_kernel, heads, req_dev, score_scale, peers),
        in_specs=[vmem] * 10,
        out_specs=[vmem] * 2,
        out_shape=[
            jax.ShapeDtypeStruct(message(rows, peers), bf16),
            jax.ShapeDtypeStruct((kv_local, pages_dev, head_size), f32),
        ],
        scratch_shapes=[
            pltpu.VMEM((rows, slots), f32),
            pltpu.VMEM((rows, head_size), f32),
        ],
        compiler_params=pltpu.CompilerParams(vmem_limit_bytes=24 << 20),
        name="attend",
    )(
        keys, kept, fold_mass, share, fold_key, target, slot, values, *near, *far,
    )


def combine_kernel(
    heads, kv_local, req_dev, score_scale, kv_count, peers, rank_ref, query_ref, fresh_ref,
    weight_ref, *rest
):
    got_ref, attended_ref, *out_refs = rest
    got = got_ref[...]
    if got.shape[1] == 128:
        size = got.shape[0] // peers
        each = size * 4 // 5
        got = got.astype(f32)
        own_rows, stat_rows = [], []
        for n in range(peers):
            own_rows.append(got[n * size : n * size + each])
            together = got[n * size + each : (n + 1) * size]
            stat_rows += [together] + [jnp.roll(together, 128 - 32 * k, axis=1) for k in range(1, 4)]
        got = jnp.concatenate(
            [jnp.concatenate(own_rows, axis=0), jnp.concatenate(stat_rows, axis=0)], axis=1
        ).astype(bf16)
    rows = got.shape[0]
    cols = heads * req_dev
    width = weight_ref.shape[1] // kv_count
    stats = got[:, 128:].astype(f32)
    top = stats[:, 0:1] + stats[:, 1:2] + stats[:, 2:3]
    request = stats[:, 6:7]
    row_head = (iota((rows, cols), 0) % heads).astype(f32)
    col = iota((rows, cols), 1)
    match = jnp.logical_and(
        request == (col % req_dev).astype(f32), row_head == (col // req_dev).astype(f32)
    )
    head, request = iota((cols, 1), 0) // req_dev, iota((cols, 1), 0) % req_dev

    def rows_of(ref, index):
        return dot(ones_where(iota((cols, ref.shape[0]), 1) == index), ref[...])

    fresh_row = request * (2 * kv_local) + head // (heads // kv_local)
    own = jnp.sum(
        rows_of(query_ref, request * heads + head) * rows_of(fresh_ref, fresh_row),
        axis=1, keepdims=True,
    ) * score_scale
    diagonal = iota((cols, cols), 0) == iota((cols, cols), 1)
    own_row = jnp.sum(jnp.where(diagonal, own, 0.0), axis=0, keepdims=True)
    best = jnp.maximum(
        jnp.max(jnp.where(match, top, negative_floor), axis=0, keepdims=True), own_row
    )
    best_col = jnp.sum(jnp.where(diagonal, best, 0.0), axis=1, keepdims=True)
    factor = jnp.where(match, jnp.exp(top - best), 0.0)
    high, middle, low = pieces(factor)
    sums = dot(high, got, (0, 0)) + dot(middle, got, (0, 0)) + dot(low, got, (0, 0))
    own_factor = jnp.exp(own - best_col)
    denominator = sums[:, 131:132] + sums[:, 132:133] + sums[:, 133:134] + own_factor
    numerator = sums[:, :128] + own_factor * rows_of(fresh_ref, fresh_row + kv_local)
    attended = numerator / denominator
    attended = jnp.concatenate(
        [attended[h * req_dev : (h + 1) * req_dev] for h in range(heads)], axis=1
    ).astype(bf16)
    attended_ref[...] = attended
    rank = rank_ref[0]
    for k in range(kv_count):
        other = jnp.bitwise_xor(rank, k)
        at = pl.multiple_of(other * width, width)
        out_refs[k][...] = dot(attended, weight_ref[:, pl.ds(at, width)]).astype(bf16)


def combine(rank, got, query, fresh, out_weight, score_scale, heads, kv_local, kv_count, peers):
    req_dev = query.shape[0] // heads
    vmem = pl.BlockSpec(memory_space=pltpu.VMEM)
    smem = pl.BlockSpec(memory_space=pltpu.SMEM)
    width = out_weight.shape[1] // kv_count
    return pl.pallas_call(
        functools.partial(combine_kernel, heads, kv_local, req_dev, score_scale, kv_count, peers),
        in_specs=[smem] + [vmem] * 4,
        out_specs=[vmem] * (1 + kv_count),
        out_shape=[jax.ShapeDtypeStruct((req_dev, out_weight.shape[0]), bf16)]
        + [jax.ShapeDtypeStruct((req_dev, width), bf16)] * kv_count,
        compiler_params=pltpu.CompilerParams(vmem_limit_bytes=24 << 20),
        cost_estimate=pl.CostEstimate(
            flops=2 * req_dev * out_weight.size, bytes_accessed=2 * out_weight.size, transcendentals=0
        ),
        name="combine",
    )(rank, query, fresh, out_weight, got)


def exchange(x, axis, count, mask):
    return lax.ppermute(x, axis, [(i, i ^ mask) for i in range(count)])


def shift(x, axis, count, step):
    return lax.ppermute(x, axis, [(i, (i + step) % count) for i in range(count)])


def per_device(
    page_cache, keep_list, fold_weight, page_table, lengths, queries, fresh_entries, out_weight
):
    seq_count = lax.axis_size("seq")
    kv_count = lax.axis_size("kv")
    assert seq_count & (seq_count - 1) == 0 and kv_count & (kv_count - 1) == 0
    seq_rank = lax.axis_index("seq").astype(i32).reshape(1)
    kv_rank = lax.axis_index("kv").astype(i32).reshape(1)
    _, _, kv_local, slots, head_size = page_cache.shape
    req_dev, heads, _ = queries.shape
    score_scale = head_size ** (-0.5)

    others = {k: shift(queries, "seq", seq_count, 2 * k) for k in [2] + [k for k in range(seq_count // 2 - 1, 0, -1) if k != 2]}
    others = [others[k] for k in range(1, seq_count // 2)]
    keys, values, own, fresh, mass, kept, fold_mass, position, count, share, target, slot = prepare(
        seq_rank, page_table, lengths, keep_list, fold_weight, queries, fresh_entries, page_cache,
        heads, req_dev,
    )
    flat = lambda x: x.reshape(-1, head_size)
    own, *others = lax.optimization_barrier((own, *others))
    near = [jnp.concatenate([flat(x) for x in [own] + others])]
    far = [exchange(near[0], "seq", seq_count, 1)]
    fold_key, keys = fold_keys(keys, share)
    fold_key, *far = lax.optimization_barrier((fold_key, *far))
    send, fold_value = attend(
        near, far, keys, kept, fold_mass, share, fold_key, target, slot, values, score_scale,
        heads, req_dev, seq_count,
    )
    got = lax.all_to_all(
        send.reshape(seq_count, -1, send.shape[1]), "seq", split_axis=0, concat_axis=0, tiled=True
    ).reshape(send.shape)
    pages_dev = page_cache.shape[0]
    fold_key, fold_value = lax.optimization_barrier((fold_key, fold_value))
    middle = pages_dev // 2
    packed = pack(
        "pack_first", [(0, 0, pages_dev), (1, 0, middle)], page_cache, position, count, fold_key,
        fold_value,
    )
    got, packed = lax.optimization_barrier((got, packed))
    attended, *shares = combine(
        kv_rank, got, flat(own), flat(fresh), out_weight, score_scale, heads, kv_local, kv_count,
        seq_count,
    )
    packed, *shares = lax.optimization_barrier((packed, *shares))
    packed = pack(
        "pack_rest", [(1, middle, pages_dev)], page_cache, position, count, fold_key, fold_value, packed
    )
    total = shares[0].astype(f32)
    for k in range(kv_count - 1, 0, -1):
        total = total + exchange(shares[k], "kv", kv_count, k).astype(f32)
    return packed, mass, attended, total.astype(bf16)


def solution(mesh):
    placed = (
        P("seq", None, "kv", None, None),
        P("seq", None),
        P("seq", None),
        P(),
        P(),
        P("seq", "kv", None),
        P("seq", None, "kv", None),
        P("kv", None),
    )
    return jax.shard_map(
        per_device,
        mesh=mesh,
        in_specs=placed,
        out_specs=(
            P("seq", None, "kv", None, None),
            P("seq", None),
            P("seq", "kv"),
            P("seq", "kv"),
        ),
        check_vma=False,
    )
```

```python
import functools

import jax
import jax.numpy as jnp
from jax import lax
from jax.experimental import pallas as pl
from jax.experimental.pallas import tpu as pltpu
from jax.sharding import PartitionSpec as P

negative_floor = -1e30
f32 = jnp.float32
bf16 = jnp.bfloat16
i32 = jnp.int32


def iota(shape, dim):
    return lax.broadcasted_iota(i32, shape, dim)


def dot(a, b, contract=(1, 0)):
    return lax.dot_general(
        a, b, (((contract[0],), (contract[1],)), ((), ())), preferred_element_type=f32
    )


def pieces(x):
    high = x.astype(bf16)
    rest = x - high.astype(f32)
    middle = rest.astype(bf16)
    low = (rest - middle.astype(f32)).astype(bf16)
    return high, middle, low


def ones_where(mask):
    return jnp.where(mask, 1.0, 0.0).astype(bf16)


def spread_rows(pages_dev, heads):
    rows = pages_dev * heads
    return ones_where(iota((rows, pages_dev), 0) // heads == iota((rows, pages_dev), 1))


def select_left(page, position, count_ref, slots):
    row = iota((slots, slots), 0).astype(f32)
    selector = ones_where(row == position[pl.ds(page, 1), :])
    return selector, row == count_ref[pl.ds(page, 1), :]


def share_rows(page, share):
    row = iota((16, share.shape[2]), 0)
    rows = jnp.zeros((16, share.shape[2]), f32)
    for n in range(3):
        rows = jnp.where(row == n, share[n, pl.ds(page, 1), :], rows)
    return rows.astype(bf16)


def rounded_fold(rows):
    return jnp.sum(rows, axis=0, keepdims=True).astype(bf16).astype(f32)


def side_by_side(ref, page):
    return jnp.concatenate([ref[page, g] for g in range(ref.shape[1])], axis=1)


def prepare_kernel(
    heads, req_dev, chunk, rank_ref, table_hbm, lengths_hbm, keep_hbm, weight_hbm, query_hbm,
    fresh_hbm, pages_hbm, keys, values, query_ref, fresh_ref, mass_ref, kept_ref, fold_mass_ref, position_ref, count_ref, share_ref,
    target_ref, slot_ref,
    table_ref, lengths_ref, keep_ref, weight_ref, small_sem, in_sem,
):
    pages_dev, slots = keep_ref.shape
    max_pages, reqs = table_ref.shape
    kv_local = keys.shape[1]
    chunks = pages_dev // chunk
    small = [
        pltpu.make_async_copy(a, b, small_sem.at[n])
        for n, (a, b) in enumerate(
            ((table_hbm, table_ref), (lengths_hbm, lengths_ref), (keep_hbm, keep_ref),
             (weight_hbm, weight_ref), (query_hbm, query_ref), (fresh_hbm, fresh_ref))
        )
    ]
    for copy in small:
        copy.start()
    loads = [
        pltpu.make_async_copy(
            pages_hbm.at[pl.ds(n * chunk, chunk), half], held.at[pl.ds(n * chunk, chunk)],
            in_sem.at[half, n],
        )
        for half, held in enumerate((keys, values))
        for n in range(held.shape[0] // chunk)
    ]
    for copy in loads:
        copy.start()
    for copy in small:
        copy.wait()

    rank = rank_ref[0]
    page_id = iota((pages_dev, reqs), 0) + rank * pages_dev
    req_id = iota((pages_dev, reqs), 1)
    valid = jnp.zeros((pages_dev, reqs), i32)
    request = jnp.zeros((pages_dev, reqs), i32)
    for j in range(max_pages):
        match = table_ref[j : j + 1, :] == page_id
        left = jnp.clip(lengths_ref[...] - j * slots, 0, slots)
        valid = valid + jnp.where(match, left, 0)
        request = request + jnp.where(match, req_id, 0)
    valid = jnp.sum(valid, axis=1, keepdims=True)
    request = jnp.sum(request, axis=1, keepdims=True)
    slot_index = iota((pages_dev, slots), 1)
    in_page = slot_index < valid
    kept = jnp.logical_and(in_page, keep_ref[...] > 0)
    dropped = jnp.logical_and(in_page, keep_ref[...] == 0)
    kept_f = jnp.where(kept, 1.0, 0.0)
    before = ones_where(iota((slots, slots), 0) < iota((slots, slots), 1))
    position = dot(kept_f.astype(bf16), before)
    count = jnp.sum(kept_f, axis=1, keepdims=True)
    dropped_weight = jnp.where(dropped, weight_ref[...], 0.0)
    weight_sum = jnp.sum(dropped_weight, axis=1, keepdims=True)
    slot_f = slot_index.astype(f32)
    mass_ref[...] = jnp.where(
        slot_f < count, 1.0, jnp.where(slot_f == count, weight_sum, 0.0)
    ).astype(bf16)
    kept_ref[...] = kept_f
    fold_mass_ref[...] = jnp.broadcast_to(weight_sum.astype(bf16).astype(f32), (pages_dev, slots))
    position_ref[...] = jnp.where(kept, position, -1.0)
    count_ref[...] = jnp.broadcast_to(count, (pages_dev, slots))
    share = pieces(dropped_weight / jnp.maximum(weight_sum, 1.0))
    for n in range(3):
        share_ref[n] = share[n].astype(f32)

    owner = request // req_dev
    chip, core = owner // 2, owner % 2
    chips = reqs // req_dev // 2
    from_chip = lax.rem(rank // 2 - chip + chips, chips)
    from_core = jnp.where(core == rank % 2, 0, 1)
    at_hand = (from_core * (reqs // req_dev // 2) + from_chip) * req_dev + request % req_dev
    at_hand = jnp.broadcast_to(at_hand, (pages_dev, slots)).astype(f32)
    spread = spread_rows(pages_dev, heads)
    rows = pages_dev * heads
    target_ref[...] = dot(spread, at_hand.astype(bf16)).astype(i32) * heads + iota((rows, slots), 0) % heads
    owner_col = jnp.broadcast_to(owner, (pages_dev, pages_dev))
    page_row, page_col = iota((pages_dev, pages_dev), 0), iota((pages_dev, pages_dev), 1)
    owner_row = jnp.sum(jnp.where(page_row == page_col, owner_col, 0), axis=0, keepdims=True)
    earlier = jnp.logical_and(owner_col == owner_row, page_row < page_col)
    order = jnp.sum(jnp.where(earlier, 1, 0), axis=0, keepdims=True)
    slot = owner_row * (pages_dev // (reqs // req_dev)) + order
    slot = jnp.broadcast_to(slot, (8, pages_dev)).astype(f32).astype(bf16)
    slot_ref[...] = dot(slot, spread, (1, 1))

    for copy in loads:
        copy.wait()


def prepare(rank, page_table, lengths, keep_list, fold_weight, queries, fresh_entries, page_cache, heads, req_dev, chunk=16):
    pages_dev, _, kv_local, slots, head_size = page_cache.shape
    reqs, max_pages = page_table.shape
    rows = pages_dev * heads
    chunks = pages_dev // chunk
    hbm = pl.BlockSpec(memory_space=pltpu.HBM)
    vmem = pl.BlockSpec(memory_space=pltpu.VMEM)
    small = (pages_dev, slots)
    return pl.pallas_call(
        functools.partial(prepare_kernel, heads, req_dev, chunk),
        in_specs=[pl.BlockSpec(memory_space=pltpu.SMEM)] + [hbm] * 7,
        out_specs=[vmem] * 12,
        out_shape=[
            pltpu.VMEM((pages_dev, kv_local, slots, head_size), bf16),
            pltpu.VMEM((pages_dev, kv_local, slots, head_size), bf16),
            pltpu.VMEM(queries.shape, bf16),
            pltpu.VMEM(fresh_entries.shape, bf16),
            jax.ShapeDtypeStruct(small, bf16),
            jax.ShapeDtypeStruct(small, f32),
            jax.ShapeDtypeStruct(small, f32),
            jax.ShapeDtypeStruct(small, f32),
            jax.ShapeDtypeStruct(small, f32),
            jax.ShapeDtypeStruct((3,) + small, f32),
            jax.ShapeDtypeStruct((rows, slots), i32),
            jax.ShapeDtypeStruct((8, rows), f32),
        ],
        scratch_shapes=[
            pltpu.VMEM((max_pages, reqs), i32),
            pltpu.VMEM((1, reqs), i32),
            pltpu.VMEM(small, i32),
            pltpu.VMEM(small, f32),
            pltpu.SemaphoreType.DMA((6,)),
            pltpu.SemaphoreType.DMA((2, chunks)),
        ],
        compiler_params=pltpu.CompilerParams(vmem_limit_bytes=24 << 20),
        name="prepare",
    )(
        rank, *(
            pltpu.with_memory_space_constraint(x, pltpu.HBM)
            for x in (
                page_table.T, lengths.reshape(1, -1), keep_list, fold_weight, queries, fresh_entries,
                page_cache,
            )
        )
    )


def fold_page(page, held, share_ref, folded_ref):
    result = dot(share_rows(page, share_ref), side_by_side(held, page))
    folded = rounded_fold(result[:8])
    for g in range(held.shape[1]):
        folded_ref[g, page : page + 1, :] = folded[:, g * 128 : (g + 1) * 128]


def fold_kernel(keys, values, share_ref, fold_key_ref, fold_value_ref, *_):
    for held, folded_ref in ((keys, fold_key_ref), (values, fold_value_ref)):
        for page in range(held.shape[0]):
            fold_page(page, held, share_ref, folded_ref)


def fold(keys, values, share):
    kv_local, head_size = keys.shape[1], keys.shape[3]
    vmem = pl.BlockSpec(memory_space=pltpu.VMEM)
    return pl.pallas_call(
        fold_kernel,
        in_specs=[vmem] * 3,
        out_specs=[vmem] * 4,
        out_shape=[
            jax.ShapeDtypeStruct((kv_local, keys.shape[0], head_size), f32),
            jax.ShapeDtypeStruct((kv_local, values.shape[0], head_size), f32),
            pltpu.VMEM(keys.shape, bf16),
            pltpu.VMEM(values.shape, bf16),
        ],
        input_output_aliases={0: 2, 1: 3},
        compiler_params=pltpu.CompilerParams(vmem_limit_bytes=24 << 20),
        name="fold",
    )(keys, values, share)


def pack_kernel(spans, chunk, pages_hbm, position_ref, count_ref, *rest):
    folded_refs = rest[:2]
    packed_hbm, raw, staged, in_sem, out_sem = rest[-5:]
    slots = position_ref.shape[1]
    kv_local = raw.shape[1]
    parts = [(half, n) for half, first, end in spans for n in range(first, end, chunk)]
    loads, stores = [], []
    for i, (half, n) in enumerate(parts):
        there, here = pl.ds(n, chunk), pl.ds(i * chunk, chunk)
        loads.append(
            pltpu.make_async_copy(pages_hbm.at[there, half], raw.at[here], in_sem.at[i])
        )
        stores.append(
            pltpu.make_async_copy(staged.at[here], packed_hbm.at[there, half], out_sem.at[i])
        )
    for copy in loads:
        copy.start()
    for i, (half, n) in enumerate(parts):
        loads[i].wait()
        for j in range(chunk):
            page, at = n + j, i * chunk + j
            selector, at_fold = select_left(page, position_ref, count_ref, slots)
            result = dot(selector, side_by_side(raw, at))
            for g in range(kv_local):
                staged[at, g] = jnp.where(
                    at_fold, folded_refs[half][g, pl.ds(page, 1), :],
                    result[:, g * 128 : (g + 1) * 128],
                ).astype(bf16)
        stores[i].start()
    for copy in stores:
        copy.wait()


def pack(name, spans, page_cache, position, count, fold_key, fold_value, packed=None, chunk=8):
    _, _, kv_local, slots, head_size = page_cache.shape
    hbm = pl.BlockSpec(memory_space=pltpu.HBM)
    vmem = pl.BlockSpec(memory_space=pltpu.VMEM)
    size = sum(end - first for _, first, end in spans)
    buffer = pltpu.VMEM((size, kv_local, slots, head_size), bf16)
    chunks = pltpu.SemaphoreType.DMA((size // chunk,))
    in_hbm = lambda x: pltpu.with_memory_space_constraint(x, pltpu.HBM)
    there = [] if packed is None else [in_hbm(packed)]
    return pl.pallas_call(
        functools.partial(pack_kernel, spans, chunk),
        in_specs=[hbm] + [vmem] * 4 + [hbm] * len(there),
        out_specs=hbm,
        out_shape=jax.ShapeDtypeStruct(page_cache.shape, bf16),
        input_output_aliases={5: 0} if there else {},
        scratch_shapes=[buffer, buffer, chunks, chunks],
        compiler_params=pltpu.CompilerParams(vmem_limit_bytes=24 << 20),
        name=name,
    )(in_hbm(page_cache), position, count, fold_key, fold_value, *there)


def message(rows, peers):
    each = rows // peers
    return (peers * (each + each // 4), 128) if each % 32 == 0 else (rows, 256)


def attend_kernel(
    heads, req_dev, score_scale, peers, keys, kept_ref, fold_mass_ref,
    fold_key_ref, target_ref, slot_ref, values, fold_value_ref, *rest,
):
    pages_dev, slots = kept_ref.shape
    query_refs = rest[:2]
    out_ref, scores, parts = rest[2:]
    kv_local = keys.shape[1]
    groups = heads // kv_local
    rows = pages_dev * heads
    spread = spread_rows(pages_dev, heads)

    query = jnp.zeros((rows, 128), f32)
    held = jnp.concatenate([ref[...] for ref in query_refs], axis=0)
    for first in range(0, held.shape[0], slots):
        pick = ones_where(target_ref[...] == iota((rows, slots), 1) + first)
        query = query + dot(pick, held[first : first + slots])
    query_b = query.astype(bf16)

    tile = 16
    tile_pages = tile // heads
    row = iota((tile, 128), 0)
    row_page = row // heads
    row_group = (row % heads) // groups

    def choose(results):
        chosen = results[0][:tile, :128]
        for i in range(tile_pages):
            for g in range(kv_local):
                if i + g > 0:
                    here = jnp.logical_and(row_page == i, row_group == g)
                    chosen = jnp.where(here, results[i][:tile, g * 128 : (g + 1) * 128], chosen)
        return chosen

    for first in range(0, pages_dev, tile_pages):
        at = first * heads
        left = query_b[at : at + tile]
        results = [
            dot(left, keys[first + i].reshape(kv_local * slots, 128), (1, 1))
            for i in range(tile_pages)
        ]
        scores[at : at + tile, :] = choose(results)

    group_of = (iota((rows, pages_dev), 0) % heads) // groups
    spread_g = [
        jnp.where(group_of == g, spread.astype(f32), 0.0).astype(bf16) for g in range(kv_local)
    ]

    def spread_fold(ref):
        return sum(dot(spread_g[g], ref[g].astype(bf16)) for g in range(kv_local))

    kept = dot(spread, kept_ref[...].astype(bf16)) > 0.5
    fold_mass = dot(spread, fold_mass_ref[...].astype(bf16))[:, :1]
    fold_score = jnp.sum(query * spread_fold(fold_key_ref), axis=1, keepdims=True) * score_scale
    fold_live = fold_mass > 0
    score = jnp.where(kept, scores[...] * score_scale, negative_floor)
    top = jnp.maximum(
        jnp.max(score, axis=1, keepdims=True), jnp.where(fold_live, fold_score, negative_floor)
    )
    weight = jnp.where(kept, jnp.exp(score - top), 0.0)
    fold_weight = jnp.where(fold_live, fold_mass * jnp.exp(fold_score - top), 0.0)
    total = jnp.sum(weight, axis=1, keepdims=True) + fold_weight
    weight_b = weight.astype(bf16)

    for first in range(0, pages_dev, tile_pages):
        at = first * heads
        left = weight_b[at : at + tile]
        results = [dot(left, side_by_side(values, first + i)) for i in range(tile_pages)]
        parts[at : at + tile, :] = choose(results)

    part = parts[...] + fold_weight.astype(bf16).astype(f32) * spread_fold(fold_value_ref)
    lane = iota((rows, 128), 1)
    local = (target_ref[...] // heads % req_dev).astype(f32)
    stats = jnp.where(lane == 6, local, 0.0)
    for n, piece in enumerate(pieces(top) + pieces(total)):
        stats = jnp.where(lane == n, piece.astype(f32), stats)
    send = jnp.concatenate([part.astype(bf16), stats.astype(bf16)], axis=1)
    place = slot_ref[:1] * heads + (iota((1, rows), 1) % heads).astype(f32)
    move = ones_where(iota((rows, rows), 0).astype(f32) == place)
    placed = dot(move, send)
    each = rows // peers
    if out_ref.shape[1] == 256:
        out_ref[...] = placed.astype(bf16)
    else:
        quarter = each // 4
        message_rows = []
        for n in range(peers):
            mine = placed[n * each : (n + 1) * each]
            message_rows.append(mine[:, :128])
            message_rows.append(
                mine[:quarter, 128:]
                + sum(
                    jnp.roll(mine[k * quarter : (k + 1) * quarter, 128:], 32 * k, axis=1)
                    for k in range(1, 4)
                )
            )
        out_ref[...] = jnp.concatenate(message_rows, axis=0).astype(bf16)


def attend(
    near, far, keys, kept, fold_mass, fold_key, target, slot, values, fold_value, score_scale,
    heads, req_dev, peers
):
    pages_dev, _, slots, head_size = keys.shape
    rows = pages_dev * heads
    vmem = pl.BlockSpec(memory_space=pltpu.VMEM)
    return pl.pallas_call(
        functools.partial(attend_kernel, heads, req_dev, score_scale, peers),
        in_specs=[vmem] * 10,
        out_specs=vmem,
        out_shape=jax.ShapeDtypeStruct(message(rows, peers), bf16),
        scratch_shapes=[
            pltpu.VMEM((rows, slots), f32),
            pltpu.VMEM((rows, head_size), f32),
        ],
        compiler_params=pltpu.CompilerParams(vmem_limit_bytes=24 << 20),
        name="attend",
    )(
        keys, kept, fold_mass, fold_key, target, slot, values, fold_value, *near, *far,
    )


def combine_kernel(
    heads, kv_local, req_dev, score_scale, kv_count, peers, rank_ref, query_ref, fresh_ref,
    weight_ref, *rest
):
    got_ref, attended_ref, *out_refs = rest
    got = got_ref[...]
    if got.shape[1] == 128:
        size = got.shape[0] // peers
        each = size * 4 // 5
        got = got.astype(f32)
        own_rows, stat_rows = [], []
        for n in range(peers):
            own_rows.append(got[n * size : n * size + each])
            together = got[n * size + each : (n + 1) * size]
            stat_rows += [together] + [jnp.roll(together, 128 - 32 * k, axis=1) for k in range(1, 4)]
        got = jnp.concatenate(
            [jnp.concatenate(own_rows, axis=0), jnp.concatenate(stat_rows, axis=0)], axis=1
        ).astype(bf16)
    rows = got.shape[0]
    cols = heads * req_dev
    width = weight_ref.shape[1] // kv_count
    stats = got[:, 128:].astype(f32)
    top = stats[:, 0:1] + stats[:, 1:2] + stats[:, 2:3]
    request = stats[:, 6:7]
    row_head = (iota((rows, cols), 0) % heads).astype(f32)
    col = iota((rows, cols), 1)
    match = jnp.logical_and(
        request == (col % req_dev).astype(f32), row_head == (col // req_dev).astype(f32)
    )
    head, request = iota((cols, 1), 0) // req_dev, iota((cols, 1), 0) % req_dev

    def rows_of(ref, index):
        return dot(ones_where(iota((cols, ref.shape[0]), 1) == index), ref[...])

    fresh_row = request * (2 * kv_local) + head // (heads // kv_local)
    own = jnp.sum(
        rows_of(query_ref, request * heads + head) * rows_of(fresh_ref, fresh_row),
        axis=1, keepdims=True,
    ) * score_scale
    diagonal = iota((cols, cols), 0) == iota((cols, cols), 1)
    own_row = jnp.sum(jnp.where(diagonal, own, 0.0), axis=0, keepdims=True)
    best = jnp.maximum(
        jnp.max(jnp.where(match, top, negative_floor), axis=0, keepdims=True), own_row
    )
    best_col = jnp.sum(jnp.where(diagonal, best, 0.0), axis=1, keepdims=True)
    factor = jnp.where(match, jnp.exp(top - best), 0.0)
    high, middle, low = pieces(factor)
    sums = dot(high, got, (0, 0)) + dot(middle, got, (0, 0)) + dot(low, got, (0, 0))
    own_factor = jnp.exp(own - best_col)
    denominator = sums[:, 131:132] + sums[:, 132:133] + sums[:, 133:134] + own_factor
    numerator = sums[:, :128] + own_factor * rows_of(fresh_ref, fresh_row + kv_local)
    attended = numerator / denominator
    attended = jnp.concatenate(
        [attended[h * req_dev : (h + 1) * req_dev] for h in range(heads)], axis=1
    ).astype(bf16)
    attended_ref[...] = attended
    rank = rank_ref[0]
    for k in range(kv_count):
        other = jnp.bitwise_xor(rank, k)
        at = pl.multiple_of(other * width, width)
        out_refs[k][...] = dot(attended, weight_ref[:, pl.ds(at, width)]).astype(bf16)


def combine(rank, got, query, fresh, out_weight, score_scale, heads, kv_local, kv_count, peers):
    req_dev = query.shape[0] // heads
    vmem = pl.BlockSpec(memory_space=pltpu.VMEM)
    smem = pl.BlockSpec(memory_space=pltpu.SMEM)
    width = out_weight.shape[1] // kv_count
    return pl.pallas_call(
        functools.partial(combine_kernel, heads, kv_local, req_dev, score_scale, kv_count, peers),
        in_specs=[smem] + [vmem] * 4,
        out_specs=[vmem] * (1 + kv_count),
        out_shape=[jax.ShapeDtypeStruct((req_dev, out_weight.shape[0]), bf16)]
        + [jax.ShapeDtypeStruct((req_dev, width), bf16)] * kv_count,
        compiler_params=pltpu.CompilerParams(vmem_limit_bytes=24 << 20),
        cost_estimate=pl.CostEstimate(
            flops=2 * req_dev * out_weight.size, bytes_accessed=2 * out_weight.size, transcendentals=0
        ),
        name="combine",
    )(rank, query, fresh, out_weight, got)


def exchange(x, axis, count, mask):
    return lax.ppermute(x, axis, [(i, i ^ mask) for i in range(count)])


def shift(x, axis, count, step):
    return lax.ppermute(x, axis, [(i, (i + step) % count) for i in range(count)])


def per_device(
    page_cache, keep_list, fold_weight, page_table, lengths, queries, fresh_entries, out_weight
):
    seq_count = lax.axis_size("seq")
    kv_count = lax.axis_size("kv")
    assert seq_count & (seq_count - 1) == 0 and kv_count & (kv_count - 1) == 0
    seq_rank = lax.axis_index("seq").astype(i32).reshape(1)
    kv_rank = lax.axis_index("kv").astype(i32).reshape(1)
    _, _, kv_local, slots, head_size = page_cache.shape
    req_dev, heads, _ = queries.shape
    score_scale = head_size ** (-0.5)

    others = {k: shift(queries, "seq", seq_count, 2 * k) for k in [2] + [k for k in range(seq_count // 2 - 1, 0, -1) if k != 2]}
    others = [others[k] for k in range(1, seq_count // 2)]
    keys, values, own, fresh, mass, kept, fold_mass, position, count, share, target, slot = prepare(
        seq_rank, page_table, lengths, keep_list, fold_weight, queries, fresh_entries, page_cache,
        heads, req_dev,
    )
    flat = lambda x: x.reshape(-1, head_size)
    own, *others = lax.optimization_barrier((own, *others))
    near = [jnp.concatenate([flat(x) for x in [own] + others])]
    far = [exchange(near[0], "seq", seq_count, 1)]
    fold_key, fold_value, keys, values = fold(keys, values, share)
    fold_key, *far = lax.optimization_barrier((fold_key, *far))
    send = attend(
        near, far, keys, kept, fold_mass, fold_key, target, slot, values, fold_value, score_scale,
        heads, req_dev, seq_count,
    )
    got = lax.all_to_all(
        send.reshape(seq_count, -1, send.shape[1]), "seq", split_axis=0, concat_axis=0, tiled=True
    ).reshape(send.shape)
    pages_dev = page_cache.shape[0]
    fold_key, send = lax.optimization_barrier((fold_key, send))
    middle = pages_dev // 2
    packed = pack(
        "pack_first", [(0, 0, pages_dev), (1, 0, middle)], page_cache, position, count, fold_key,
        fold_value,
    )
    got, packed = lax.optimization_barrier((got, packed))
    attended, *shares = combine(
        kv_rank, got, flat(own), flat(fresh), out_weight, score_scale, heads, kv_local, kv_count,
        seq_count,
    )
    packed, *shares = lax.optimization_barrier((packed, *shares))
    packed = pack(
        "pack_rest", [(1, middle, pages_dev)], page_cache, position, count, fold_key, fold_value, packed
    )
    total = shares[0].astype(f32)
    for k in range(1, kv_count):
        total = total + exchange(shares[k], "kv", kv_count, k).astype(f32)
    return packed, mass, attended, total.astype(bf16)


def solution(mesh):
    placed = (
        P("seq", None, "kv", None, None),
        P("seq", None),
        P("seq", None),
        P(),
        P(),
        P("seq", "kv", None),
        P("seq", None, "kv", None),
        P("kv", None),
    )
    return jax.shard_map(
        per_device,
        mesh=mesh,
        in_specs=placed,
        out_specs=(
            P("seq", None, "kv", None, None),
            P("seq", None),
            P("seq", "kv"),
            P("seq", "kv"),
        ),
        check_vma=False,
    )
```

```python
import functools

import jax
import jax.numpy as jnp
from jax import lax
from jax.experimental import pallas as pl
from jax.experimental.pallas import tpu as pltpu
from jax.sharding import PartitionSpec as P

negative_floor = -1e30
f32 = jnp.float32
bf16 = jnp.bfloat16
i32 = jnp.int32


def iota(shape, dim):
    return lax.broadcasted_iota(i32, shape, dim)


def dot(a, b, contract=(1, 0)):
    return lax.dot_general(
        a, b, (((contract[0],), (contract[1],)), ((), ())), preferred_element_type=f32
    )


def pieces(x):
    high = x.astype(bf16)
    rest = x - high.astype(f32)
    middle = rest.astype(bf16)
    low = (rest - middle.astype(f32)).astype(bf16)
    return high, middle, low


def ones_where(mask):
    return jnp.where(mask, 1.0, 0.0).astype(bf16)


def spread_rows(pages_dev, heads):
    rows = pages_dev * heads
    return ones_where(iota((rows, pages_dev), 0) // heads == iota((rows, pages_dev), 1))


def select_left(page, position, count_ref, slots):
    row = iota((slots, slots), 0).astype(f32)
    selector = ones_where(row == position[pl.ds(page, 1), :])
    return selector, row == count_ref[pl.ds(page, 1), :]


def share_rows(page, share):
    row = iota((16, share.shape[2]), 0)
    rows = jnp.zeros((16, share.shape[2]), f32)
    for n in range(3):
        rows = jnp.where(row == n, share[n, pl.ds(page, 1), :], rows)
    return rows.astype(bf16)


def rounded_fold(rows):
    return jnp.sum(rows, axis=0, keepdims=True).astype(bf16).astype(f32)


def side_by_side(ref, page):
    return jnp.concatenate([ref[page, g] for g in range(ref.shape[1])], axis=1)


def prepare_kernel(
    heads, req_dev, chunk, rank_ref, table_hbm, lengths_hbm, keep_hbm, weight_hbm, query_hbm,
    fresh_hbm, pages_hbm, keys, values, query_ref, fresh_ref, mass_ref, kept_ref, fold_mass_ref, position_ref, count_ref, share_ref,
    target_ref, slot_ref,
    table_ref, lengths_ref, keep_ref, weight_ref, small_sem, in_sem,
):
    pages_dev, slots = keep_ref.shape
    max_pages, reqs = table_ref.shape
    kv_local = keys.shape[1]
    chunks = pages_dev // chunk
    small = [
        pltpu.make_async_copy(a, b, small_sem.at[n])
        for n, (a, b) in enumerate(
            ((table_hbm, table_ref), (lengths_hbm, lengths_ref), (keep_hbm, keep_ref),
             (weight_hbm, weight_ref), (query_hbm, query_ref), (fresh_hbm, fresh_ref))
        )
    ]
    for copy in small:
        copy.start()
    loads = [
        pltpu.make_async_copy(
            pages_hbm.at[pl.ds(n * chunk, chunk), half], held.at[pl.ds(n * chunk, chunk)],
            in_sem.at[half, n],
        )
        for half, held in enumerate((keys, values))
        for n in range(held.shape[0] // chunk)
    ]
    for copy in loads:
        copy.start()
    for copy in small:
        copy.wait()

    rank = rank_ref[0]
    page_id = iota((pages_dev, reqs), 0) + rank * pages_dev
    req_id = iota((pages_dev, reqs), 1)
    valid = jnp.zeros((pages_dev, reqs), i32)
    request = jnp.zeros((pages_dev, reqs), i32)
    for j in range(max_pages):
        match = table_ref[j : j + 1, :] == page_id
        left = jnp.clip(lengths_ref[...] - j * slots, 0, slots)
        valid = valid + jnp.where(match, left, 0)
        request = request + jnp.where(match, req_id, 0)
    valid = jnp.sum(valid, axis=1, keepdims=True)
    request = jnp.sum(request, axis=1, keepdims=True)
    slot_index = iota((pages_dev, slots), 1)
    in_page = slot_index < valid
    kept = jnp.logical_and(in_page, keep_ref[...] > 0)
    dropped = jnp.logical_and(in_page, keep_ref[...] == 0)
    kept_f = jnp.where(kept, 1.0, 0.0)
    before = ones_where(iota((slots, slots), 0) < iota((slots, slots), 1))
    position = dot(kept_f.astype(bf16), before)
    count = jnp.sum(kept_f, axis=1, keepdims=True)
    dropped_weight = jnp.where(dropped, weight_ref[...], 0.0)
    weight_sum = jnp.sum(dropped_weight, axis=1, keepdims=True)
    slot_f = slot_index.astype(f32)
    mass_ref[...] = jnp.where(
        slot_f < count, 1.0, jnp.where(slot_f == count, weight_sum, 0.0)
    ).astype(bf16)
    kept_ref[...] = kept_f
    fold_mass_ref[...] = jnp.broadcast_to(weight_sum.astype(bf16).astype(f32), (pages_dev, slots))
    position_ref[...] = jnp.where(kept, position, -1.0)
    count_ref[...] = jnp.broadcast_to(count, (pages_dev, slots))
    share = pieces(dropped_weight / jnp.maximum(weight_sum, 1.0))
    for n in range(3):
        share_ref[n] = share[n].astype(f32)

    owner = request // req_dev
    chip, core = owner // 2, owner % 2
    chips = reqs // req_dev // 2
    from_chip = lax.rem(rank // 2 - chip + chips, chips)
    from_core = jnp.where(core == rank % 2, 0, 1)
    at_hand = (from_core * (reqs // req_dev // 2) + from_chip) * req_dev + request % req_dev
    at_hand = jnp.broadcast_to(at_hand, (pages_dev, slots)).astype(f32)
    spread = spread_rows(pages_dev, heads)
    rows = pages_dev * heads
    target_ref[...] = dot(spread, at_hand.astype(bf16)).astype(i32) * heads + iota((rows, slots), 0) % heads
    owner_col = jnp.broadcast_to(owner, (pages_dev, pages_dev))
    page_row, page_col = iota((pages_dev, pages_dev), 0), iota((pages_dev, pages_dev), 1)
    owner_row = jnp.sum(jnp.where(page_row == page_col, owner_col, 0), axis=0, keepdims=True)
    earlier = jnp.logical_and(owner_col == owner_row, page_row < page_col)
    order = jnp.sum(jnp.where(earlier, 1, 0), axis=0, keepdims=True)
    slot = owner_row * (pages_dev // (reqs // req_dev)) + order
    slot = jnp.broadcast_to(slot, (8, pages_dev)).astype(f32).astype(bf16)
    slot_ref[...] = dot(slot, spread, (1, 1))

    for copy in loads:
        copy.wait()


def prepare(rank, page_table, lengths, keep_list, fold_weight, queries, fresh_entries, page_cache, heads, req_dev, chunk=16):
    pages_dev, _, kv_local, slots, head_size = page_cache.shape
    reqs, max_pages = page_table.shape
    rows = pages_dev * heads
    chunks = pages_dev // chunk
    hbm = pl.BlockSpec(memory_space=pltpu.HBM)
    vmem = pl.BlockSpec(memory_space=pltpu.VMEM)
    small = (pages_dev, slots)
    return pl.pallas_call(
        functools.partial(prepare_kernel, heads, req_dev, chunk),
        in_specs=[pl.BlockSpec(memory_space=pltpu.SMEM)] + [hbm] * 7,
        out_specs=[vmem] * 12,
        out_shape=[
            pltpu.VMEM((pages_dev, kv_local, slots, head_size), bf16),
            pltpu.VMEM((pages_dev, kv_local, slots, head_size), bf16),
            pltpu.VMEM(queries.shape, bf16),
            pltpu.VMEM(fresh_entries.shape, bf16),
            jax.ShapeDtypeStruct(small, bf16),
            jax.ShapeDtypeStruct(small, f32),
            jax.ShapeDtypeStruct(small, f32),
            jax.ShapeDtypeStruct(small, f32),
            jax.ShapeDtypeStruct(small, f32),
            jax.ShapeDtypeStruct((3,) + small, f32),
            jax.ShapeDtypeStruct((rows, slots), i32),
            jax.ShapeDtypeStruct((8, rows), f32),
        ],
        scratch_shapes=[
            pltpu.VMEM((max_pages, reqs), i32),
            pltpu.VMEM((1, reqs), i32),
            pltpu.VMEM(small, i32),
            pltpu.VMEM(small, f32),
            pltpu.SemaphoreType.DMA((6,)),
            pltpu.SemaphoreType.DMA((2, chunks)),
        ],
        compiler_params=pltpu.CompilerParams(vmem_limit_bytes=24 << 20),
        name="prepare",
    )(
        rank, *(
            pltpu.with_memory_space_constraint(x, pltpu.HBM)
            for x in (
                page_table.T, lengths.reshape(1, -1), keep_list, fold_weight, queries, fresh_entries,
                page_cache,
            )
        )
    )


def fold_page(page, held, share_ref, folded_ref):
    result = dot(share_rows(page, share_ref), side_by_side(held, page))
    folded = rounded_fold(result[:8])
    for g in range(held.shape[1]):
        folded_ref[g, page : page + 1, :] = folded[:, g * 128 : (g + 1) * 128]


def fold_kernel(keys, values, share_ref, fold_key_ref, fold_value_ref, *_):
    for held, folded_ref in ((keys, fold_key_ref), (values, fold_value_ref)):
        for page in range(held.shape[0]):
            fold_page(page, held, share_ref, folded_ref)


def fold(keys, values, share):
    kv_local, head_size = keys.shape[1], keys.shape[3]
    vmem = pl.BlockSpec(memory_space=pltpu.VMEM)
    return pl.pallas_call(
        fold_kernel,
        in_specs=[vmem] * 3,
        out_specs=[vmem] * 4,
        out_shape=[
            jax.ShapeDtypeStruct((kv_local, keys.shape[0], head_size), f32),
            jax.ShapeDtypeStruct((kv_local, values.shape[0], head_size), f32),
            pltpu.VMEM(keys.shape, bf16),
            pltpu.VMEM(values.shape, bf16),
        ],
        input_output_aliases={0: 2, 1: 3},
        compiler_params=pltpu.CompilerParams(vmem_limit_bytes=24 << 20),
        name="fold",
    )(keys, values, share)


def pack_kernel(spans, chunk, pages_hbm, position_ref, count_ref, *rest):
    folded_refs = rest[:2]
    packed_hbm, raw, staged, in_sem, out_sem = rest[-5:]
    slots = position_ref.shape[1]
    kv_local = raw.shape[1]
    parts = [(half, n) for half, first, end in spans for n in range(first, end, chunk)]
    loads, stores = [], []
    for i, (half, n) in enumerate(parts):
        there, here = pl.ds(n, chunk), pl.ds(i * chunk, chunk)
        loads.append(
            pltpu.make_async_copy(pages_hbm.at[there, half], raw.at[here], in_sem.at[i])
        )
        stores.append(
            pltpu.make_async_copy(staged.at[here], packed_hbm.at[there, half], out_sem.at[i])
        )
    for copy in loads:
        copy.start()
    for i, (half, n) in enumerate(parts):
        loads[i].wait()
        for j in range(chunk):
            page, at = n + j, i * chunk + j
            selector, at_fold = select_left(page, position_ref, count_ref, slots)
            result = dot(selector, side_by_side(raw, at))
            for g in range(kv_local):
                staged[at, g] = jnp.where(
                    at_fold, folded_refs[half][g, pl.ds(page, 1), :],
                    result[:, g * 128 : (g + 1) * 128],
                ).astype(bf16)
        stores[i].start()
    for copy in stores:
        copy.wait()


def pack(name, spans, page_cache, position, count, fold_key, fold_value, packed=None, chunk=8):
    _, _, kv_local, slots, head_size = page_cache.shape
    hbm = pl.BlockSpec(memory_space=pltpu.HBM)
    vmem = pl.BlockSpec(memory_space=pltpu.VMEM)
    size = sum(end - first for _, first, end in spans)
    buffer = pltpu.VMEM((size, kv_local, slots, head_size), bf16)
    chunks = pltpu.SemaphoreType.DMA((size // chunk,))
    in_hbm = lambda x: pltpu.with_memory_space_constraint(x, pltpu.HBM)
    there = [] if packed is None else [in_hbm(packed)]
    return pl.pallas_call(
        functools.partial(pack_kernel, spans, chunk),
        in_specs=[hbm] + [vmem] * 4 + [hbm] * len(there),
        out_specs=hbm,
        out_shape=jax.ShapeDtypeStruct(page_cache.shape, bf16),
        input_output_aliases={5: 0} if there else {},
        scratch_shapes=[buffer, buffer, chunks, chunks],
        compiler_params=pltpu.CompilerParams(vmem_limit_bytes=24 << 20),
        name=name,
    )(in_hbm(page_cache), position, count, fold_key, fold_value, *there)


def message(rows, peers):
    each = rows // peers
    return (peers * (each + each // 4), 128) if each % 32 == 0 else (rows, 256)


def attend_kernel(
    heads, req_dev, score_scale, peers, keys, kept_ref, fold_mass_ref,
    fold_key_ref, target_ref, slot_ref, values, fold_value_ref, *rest,
):
    pages_dev, slots = kept_ref.shape
    query_refs = rest[:2]
    out_ref, scores, parts = rest[2:]
    kv_local = keys.shape[1]
    groups = heads // kv_local
    rows = pages_dev * heads
    spread = spread_rows(pages_dev, heads)

    query = jnp.zeros((rows, 128), f32)
    held = jnp.concatenate([ref[...] for ref in query_refs], axis=0)
    for first in range(0, held.shape[0], slots):
        pick = ones_where(target_ref[...] == iota((rows, slots), 1) + first)
        query = query + dot(pick, held[first : first + slots])
    query_b = query.astype(bf16)

    tile = 16
    tile_pages = tile // heads
    row = iota((tile, 128), 0)
    row_page = row // heads
    row_group = (row % heads) // groups

    def choose(results):
        chosen = results[0][:tile, :128]
        for i in range(tile_pages):
            for g in range(kv_local):
                if i + g > 0:
                    here = jnp.logical_and(row_page == i, row_group == g)
                    chosen = jnp.where(here, results[i][:tile, g * 128 : (g + 1) * 128], chosen)
        return chosen

    for first in range(0, pages_dev, tile_pages):
        at = first * heads
        left = query_b[at : at + tile]
        results = [
            dot(left, keys[first + i].reshape(kv_local * slots, 128), (1, 1))
            for i in range(tile_pages)
        ]
        scores[at : at + tile, :] = choose(results)

    group_of = (iota((rows, pages_dev), 0) % heads) // groups
    spread_g = [
        jnp.where(group_of == g, spread.astype(f32), 0.0).astype(bf16) for g in range(kv_local)
    ]

    def spread_fold(ref):
        return sum(dot(spread_g[g], ref[g].astype(bf16)) for g in range(kv_local))

    kept = dot(spread, kept_ref[...].astype(bf16)) > 0.5
    fold_mass = dot(spread, fold_mass_ref[...].astype(bf16))[:, :1]
    fold_score = jnp.sum(query * spread_fold(fold_key_ref), axis=1, keepdims=True) * score_scale
    fold_live = fold_mass > 0
    score = jnp.where(kept, scores[...] * score_scale, negative_floor)
    top = jnp.maximum(
        jnp.max(score, axis=1, keepdims=True), jnp.where(fold_live, fold_score, negative_floor)
    )
    weight = jnp.where(kept, jnp.exp(score - top), 0.0)
    fold_weight = jnp.where(fold_live, fold_mass * jnp.exp(fold_score - top), 0.0)
    total = jnp.sum(weight, axis=1, keepdims=True) + fold_weight
    weight_b = weight.astype(bf16)

    for first in range(0, pages_dev, tile_pages):
        at = first * heads
        left = weight_b[at : at + tile]
        results = [dot(left, side_by_side(values, first + i)) for i in range(tile_pages)]
        parts[at : at + tile, :] = choose(results)

    part = parts[...] + fold_weight.astype(bf16).astype(f32) * spread_fold(fold_value_ref)
    lane = iota((rows, 128), 1)
    local = (target_ref[...] // heads % req_dev).astype(f32)
    stats = jnp.where(lane == 6, local, 0.0)
    for n, piece in enumerate(pieces(top) + pieces(total)):
        stats = jnp.where(lane == n, piece.astype(f32), stats)
    send = jnp.concatenate([part.astype(bf16), stats.astype(bf16)], axis=1)
    place = slot_ref[:1] * heads + (iota((1, rows), 1) % heads).astype(f32)
    move = ones_where(iota((rows, rows), 0).astype(f32) == place)
    placed = dot(move, send)
    each = rows // peers
    if out_ref.shape[1] == 256:
        out_ref[...] = placed.astype(bf16)
    else:
        quarter = each // 4
        message_rows = []
        for n in range(peers):
            mine = placed[n * each : (n + 1) * each]
            message_rows.append(mine[:, :128])
            message_rows.append(
                mine[:quarter, 128:]
                + sum(
                    jnp.roll(mine[k * quarter : (k + 1) * quarter, 128:], 32 * k, axis=1)
                    for k in range(1, 4)
                )
            )
        out_ref[...] = jnp.concatenate(message_rows, axis=0).astype(bf16)


def attend(
    near, far, keys, kept, fold_mass, fold_key, target, slot, values, fold_value, score_scale,
    heads, req_dev, peers
):
    pages_dev, _, slots, head_size = keys.shape
    rows = pages_dev * heads
    vmem = pl.BlockSpec(memory_space=pltpu.VMEM)
    return pl.pallas_call(
        functools.partial(attend_kernel, heads, req_dev, score_scale, peers),
        in_specs=[vmem] * 10,
        out_specs=vmem,
        out_shape=jax.ShapeDtypeStruct(message(rows, peers), bf16),
        scratch_shapes=[
            pltpu.VMEM((rows, slots), f32),
            pltpu.VMEM((rows, head_size), f32),
        ],
        compiler_params=pltpu.CompilerParams(vmem_limit_bytes=24 << 20),
        name="attend",
    )(
        keys, kept, fold_mass, fold_key, target, slot, values, fold_value, *near, *far,
    )


def combine_kernel(
    heads, kv_local, req_dev, score_scale, kv_count, peers, rank_ref, query_ref, fresh_ref,
    weight_ref, *rest
):
    got_ref, attended_ref, *out_refs = rest
    got = got_ref[...]
    if got.shape[1] == 128:
        size = got.shape[0] // peers
        each = size * 4 // 5
        got = got.astype(f32)
        own_rows, stat_rows = [], []
        for n in range(peers):
            own_rows.append(got[n * size : n * size + each])
            together = got[n * size + each : (n + 1) * size]
            stat_rows += [together] + [jnp.roll(together, 128 - 32 * k, axis=1) for k in range(1, 4)]
        got = jnp.concatenate(
            [jnp.concatenate(own_rows, axis=0), jnp.concatenate(stat_rows, axis=0)], axis=1
        ).astype(bf16)
    rows = got.shape[0]
    cols = heads * req_dev
    width = weight_ref.shape[1] // kv_count
    stats = got[:, 128:].astype(f32)
    top = stats[:, 0:1] + stats[:, 1:2] + stats[:, 2:3]
    request = stats[:, 6:7]
    row_head = (iota((rows, cols), 0) % heads).astype(f32)
    col = iota((rows, cols), 1)
    match = jnp.logical_and(
        request == (col % req_dev).astype(f32), row_head == (col // req_dev).astype(f32)
    )
    head, request = iota((cols, 1), 0) // req_dev, iota((cols, 1), 0) % req_dev

    def rows_of(ref, index):
        return dot(ones_where(iota((cols, ref.shape[0]), 1) == index), ref[...])

    fresh_row = request * (2 * kv_local) + head // (heads // kv_local)
    own = jnp.sum(
        rows_of(query_ref, request * heads + head) * rows_of(fresh_ref, fresh_row),
        axis=1, keepdims=True,
    ) * score_scale
    diagonal = iota((cols, cols), 0) == iota((cols, cols), 1)
    own_row = jnp.sum(jnp.where(diagonal, own, 0.0), axis=0, keepdims=True)
    best = jnp.maximum(
        jnp.max(jnp.where(match, top, negative_floor), axis=0, keepdims=True), own_row
    )
    best_col = jnp.sum(jnp.where(diagonal, best, 0.0), axis=1, keepdims=True)
    factor = jnp.where(match, jnp.exp(top - best), 0.0)
    high, middle, _ = pieces(factor)
    sums = dot(high, got, (0, 0)) + dot(middle, got, (0, 0))
    own_factor = jnp.exp(own - best_col)
    denominator = sums[:, 131:132] + sums[:, 132:133] + sums[:, 133:134] + own_factor
    numerator = sums[:, :128] + own_factor * rows_of(fresh_ref, fresh_row + kv_local)
    attended = numerator / denominator
    attended = jnp.concatenate(
        [attended[h * req_dev : (h + 1) * req_dev] for h in range(heads)], axis=1
    ).astype(bf16)
    attended_ref[...] = attended
    rank = rank_ref[0]
    for k in range(kv_count):
        other = jnp.bitwise_xor(rank, k)
        at = pl.multiple_of(other * width, width)
        out_refs[k][...] = dot(attended, weight_ref[:, pl.ds(at, width)]).astype(bf16)


def combine(rank, got, query, fresh, out_weight, score_scale, heads, kv_local, kv_count, peers):
    req_dev = query.shape[0] // heads
    vmem = pl.BlockSpec(memory_space=pltpu.VMEM)
    smem = pl.BlockSpec(memory_space=pltpu.SMEM)
    width = out_weight.shape[1] // kv_count
    return pl.pallas_call(
        functools.partial(combine_kernel, heads, kv_local, req_dev, score_scale, kv_count, peers),
        in_specs=[smem] + [vmem] * 4,
        out_specs=[vmem] * (1 + kv_count),
        out_shape=[jax.ShapeDtypeStruct((req_dev, out_weight.shape[0]), bf16)]
        + [jax.ShapeDtypeStruct((req_dev, width), bf16)] * kv_count,
        compiler_params=pltpu.CompilerParams(vmem_limit_bytes=24 << 20),
        cost_estimate=pl.CostEstimate(
            flops=2 * req_dev * out_weight.size, bytes_accessed=2 * out_weight.size, transcendentals=0
        ),
        name="combine",
    )(rank, query, fresh, out_weight, got)


def exchange(x, axis, count, mask):
    return lax.ppermute(x, axis, [(i, i ^ mask) for i in range(count)])


def shift(x, axis, count, step):
    return lax.ppermute(x, axis, [(i, (i + step) % count) for i in range(count)])


def per_device(
    page_cache, keep_list, fold_weight, page_table, lengths, queries, fresh_entries, out_weight
):
    seq_count = lax.axis_size("seq")
    kv_count = lax.axis_size("kv")
    assert seq_count & (seq_count - 1) == 0 and kv_count & (kv_count - 1) == 0
    seq_rank = lax.axis_index("seq").astype(i32).reshape(1)
    kv_rank = lax.axis_index("kv").astype(i32).reshape(1)
    _, _, kv_local, slots, head_size = page_cache.shape
    req_dev, heads, _ = queries.shape
    score_scale = head_size ** (-0.5)

    others = {k: shift(queries, "seq", seq_count, 2 * k) for k in [2] + [k for k in range(seq_count // 2 - 1, 0, -1) if k != 2]}
    others = [others[k] for k in range(1, seq_count // 2)]
    keys, values, own, fresh, mass, kept, fold_mass, position, count, share, target, slot = prepare(
        seq_rank, page_table, lengths, keep_list, fold_weight, queries, fresh_entries, page_cache,
        heads, req_dev,
    )
    flat = lambda x: x.reshape(-1, head_size)
    own, *others = lax.optimization_barrier((own, *others))
    near = [jnp.concatenate([flat(x) for x in [own] + others])]
    far = [exchange(near[0], "seq", seq_count, 1)]
    fold_key, fold_value, keys, values = fold(keys, values, share)
    fold_key, *far = lax.optimization_barrier((fold_key, *far))
    send = attend(
        near, far, keys, kept, fold_mass, fold_key, target, slot, values, fold_value, score_scale,
        heads, req_dev, seq_count,
    )
    got = lax.all_to_all(
        send.reshape(seq_count, -1, send.shape[1]), "seq", split_axis=0, concat_axis=0, tiled=True
    ).reshape(send.shape)
    pages_dev = page_cache.shape[0]
    fold_key, send = lax.optimization_barrier((fold_key, send))
    middle = pages_dev // 2
    packed = pack(
        "pack_first", [(0, 0, pages_dev), (1, 0, middle)], page_cache, position, count, fold_key,
        fold_value,
    )
    got, packed = lax.optimization_barrier((got, packed))
    attended, *shares = combine(
        kv_rank, got, flat(own), flat(fresh), out_weight, score_scale, heads, kv_local, kv_count,
        seq_count,
    )
    packed, *shares = lax.optimization_barrier((packed, *shares))
    packed = pack(
        "pack_rest", [(1, middle, pages_dev)], page_cache, position, count, fold_key, fold_value, packed
    )
    total = shares[0].astype(f32)
    for k in range(1, kv_count):
        total = total + exchange(shares[k], "kv", kv_count, k).astype(f32)
    return packed, mass, attended, total.astype(bf16)


def solution(mesh):
    placed = (
        P("seq", None, "kv", None, None),
        P("seq", None),
        P("seq", None),
        P(),
        P(),
        P("seq", "kv", None),
        P("seq", None, "kv", None),
        P("kv", None),
    )
    return jax.shard_map(
        per_device,
        mesh=mesh,
        in_specs=placed,
        out_specs=(
            P("seq", None, "kv", None, None),
            P("seq", None),
            P("seq", "kv"),
            P("seq", "kv"),
        ),
        check_vma=False,
    )
```
